32 devices in a mesh: dp: 8 (over z, y), expert: 4 (over x, core).
Axes of the slice: x: 2, y: 2, z: 4, core: 2. Of those that a mesh axis runs over, the one named last changes fastest.
Arguments:
- tokens: bfloat16 [8192, 7168], P(('dp', 'expert')), may hold values from -6 to 6
- routes: int32 [8192, 8], P(('dp', 'expert')), may hold values from 0 to 255, as said below
- slot_ids: int32 [8192, 8], P(('dp', 'expert')), may hold values from -1 to 15, as said below
- gate_weight: bfloat16 [4, 2048, 7168], P('expert', 'dp'), may hold values from -0.0625 to 0.0625
- up_weight: bfloat16 [4, 2048, 7168], P('expert', 'dp'), may hold values from -0.0625 to 0.0625
Outputs:
- input_hessian: float32 [4, 7168, 7168], P('expert', 'dp')
- down_hessian: float32 [4, 2048, 2048], P('expert', 'dp')
The draws below stay inside these ranges and needn't reach their ends.
Inputs may be any that keep to these rules, and one draw needn't show every extreme that they name: `routes`: distinct ids in each row. On each device, no window expert is named by more than 16 tokens, and in every group of 4 consecutive devices along dp+expert (one index of dp) some window expert is named by exactly 16 tokens on every one of them. Every window expert is named on every device. `slot_ids`: for a choice of a window expert: on each device, the tokens naming that expert hold the slots 0 to n - 1, each once; for ids of 4 or more the slot is -1.
All inputs are finite; a program needn't handle non-finite values.
Results may differ from the reference program's by a relative error of at most 0.0038.
Values may be sent and summed in bfloat16 or wider, within the bound.
A program may use at most 192 MiB of HBM per device.

```python
import jax
import jax.numpy as jnp
from jax import lax

D = 7168
FF = 2048
EXPERTS_ALL = 256
TOP = 8
TOK_DEV = 256
CAP = 16
EXPERTS = 4
TOKENS = 8192


def routing(key):
    blocks = TOKENS // TOK_DEV
    keys = jax.random.split(key, 5)
    index = jnp.arange(blocks, dtype=jnp.int32)
    upper = jnp.maximum(1, CAP // 3 + (CAP - CAP // 3) * index // max(blocks - 1, 1))
    lower = jnp.maximum(1, upper // 2)
    raw = jax.random.randint(keys[0], (blocks, EXPERTS), 0, 1 << 30)
    counts = raw % (upper - lower + 1)[:, None] + lower[:, None]
    full_pick = jax.random.randint(keys[1], (blocks // EXPERTS,), 0, EXPERTS)
    full_each = full_pick[index // EXPERTS]
    counts = jnp.where(jnp.arange(EXPERTS)[None, :] == full_each[:, None], CAP, counts)
    scores = jax.random.randint(keys[2], (blocks, EXPERTS, TOK_DEV), 0, 1 << 20) * TOK_DEV + jnp.arange(TOK_DEV, dtype=jnp.int32)
    ranking = jnp.argsort(jnp.argsort(scores, axis=2, stable=True), axis=2, stable=True).astype(jnp.int32)
    chosen = ranking < counts[:, :, None]
    chosen_t = jnp.transpose(chosen, (0, 2, 1))
    ranking_t = jnp.transpose(ranking, (0, 2, 1))
    others = EXPERTS_ALL - EXPERTS
    other_scores = jax.random.randint(keys[3], (blocks, TOK_DEV, others), 0, 1 << 20) * others + jnp.arange(others, dtype=jnp.int32)
    fill_ids = lax.top_k(other_scores, TOP)[1].astype(jnp.int32) + EXPERTS
    window_ids = jnp.broadcast_to(jnp.arange(EXPERTS, dtype=jnp.int32), (blocks, TOK_DEV, EXPERTS))
    cand_ids = jnp.concatenate([window_ids, fill_ids], axis=2)
    cand_slots = jnp.concatenate([ranking_t, jnp.full((blocks, TOK_DEV, TOP), -1, jnp.int32)], axis=2)
    order_key = jnp.concatenate([jnp.where(chosen_t, 0, 2), jnp.ones((blocks, TOK_DEV, TOP), jnp.int32)], axis=2)
    order = jnp.argsort(order_key, axis=2, stable=True)[:, :, :TOP]
    picked_ids = jnp.take_along_axis(cand_ids, order, axis=2)
    picked_slots = jnp.take_along_axis(cand_slots, order, axis=2)
    shuffle = jax.random.randint(keys[4], (blocks, TOK_DEV, TOP), 0, 1 << 20) * TOP + jnp.arange(TOP, dtype=jnp.int32)
    mixing = jnp.argsort(shuffle, axis=2, stable=True)
    picked_ids = jnp.take_along_axis(picked_ids, mixing, axis=2).reshape(TOKENS, TOP)
    picked_slots = jnp.take_along_axis(picked_slots, mixing, axis=2).reshape(TOKENS, TOP)
    return (picked_ids.astype(jnp.int32), picked_slots.astype(jnp.int32))


def draw_routes(key, part):
    return routing(key)[0]


def draw_slot_ids(key, part):
    return routing(key)[1]


def levels(stream_key, shape, cuts, low, top_value):
    loudness, own = 1.0, jax.random.fold_in(stream_key, 6)
    for dim, blocks in cuts:
        heights = jnp.exp(jax.random.uniform(jax.random.fold_in(own, dim), (blocks,), jnp.float32, low / len(cuts), top_value / len(cuts)))
        loudness = loudness * jnp.repeat(heights, shape[dim] // blocks).reshape([-1 if axis == dim else 1 for axis in range(len(shape))])
    return loudness


def gaussian(own_key, extent, width, bound, pieces=(), held_as=jnp.bfloat16):
    factor_of = levels(own_key, extent, pieces, -0.22, 0.18) if pieces else 1.0
    drawn = jax.random.normal(own_key, extent, jnp.float32) * width * factor_of
    return jnp.minimum(jnp.maximum(drawn, -bound), bound).astype(held_as)


def setup_inputs(seed: int = 0) -> dict:
    key_of = jax.random.split(jax.random.key(seed), 6)
    tokens = gaussian(key_of[0], (TOKENS, D), 1.0, 6.0, ((0, 32),))
    routes = draw_routes(jax.random.fold_in(key_of[5], 71), 0)
    slot_ids = draw_slot_ids(jax.random.fold_in(key_of[5], 71), 0)
    gate_weight = gaussian(key_of[3], (EXPERTS, FF, D), D ** -0.5, 0.0625, ((0, 4), (1, 8)))
    up_weight = gaussian(key_of[4], (EXPERTS, FF, D), D ** -0.5, 0.0625, ((0, 4), (1, 8)))
    return {"tokens": tokens, "routes": routes, "slot_ids": slot_ids, "gate_weight": gate_weight, "up_weight": up_weight}


def reference(tokens, routes, slot_ids, gate_weight, up_weight):
    blocks = TOKENS // TOK_DEV
    owner_block = (jnp.arange(TOKENS, dtype=jnp.int32) // TOK_DEV).astype(jnp.int32)
    hessians = []
    downs = []
    for expert_id in range(EXPERTS):
        chosen = routes == expert_id
        member = jnp.any(chosen, axis=1)
        slot_here = jnp.sum(jnp.where(chosen, slot_ids, 0), axis=1).astype(jnp.int32)
        target = jnp.where(member, owner_block * CAP + slot_here, blocks * CAP).astype(jnp.int32)
        buffer = jnp.zeros((blocks * CAP + 1, D), jnp.bfloat16).at[target].set(tokens)[: blocks * CAP]
        routed = jnp.sum(member.astype(jnp.float32))
        factor = 2.0 / routed
        gram = jnp.dot(buffer.T, buffer, preferred_element_type=jnp.float32)
        hessians.append(gram * factor)
        gate = jnp.dot(buffer, gate_weight[expert_id].T, preferred_element_type=jnp.float32)
        upward = jnp.dot(buffer, up_weight[expert_id].T, preferred_element_type=jnp.float32)
        hidden = (jax.nn.silu(gate) * upward).astype(jnp.bfloat16)
        downs.append(jnp.dot(hidden.T, hidden, preferred_element_type=jnp.float32) * factor)
    return jnp.stack(hessians), jnp.stack(downs)
```

```python
import functools

import jax
import jax.numpy as jnp
from jax import lax
from jax.experimental import pallas as pl
from jax.experimental.pallas import tpu as pltpu
from jax.sharding import PartitionSpec as P

CAP = 16
MESH = pl.DeviceIdType.MESH


def peer(e, k, owners):
    return ((e // 2 + k // 2) % (owners // 2)) * 2 + (e + k) % 2


def gather_kernel(n, owners, hot_ref, tok_ref, gate_ref, up_ref, x_ref, hid_ref,
                  xbuf, sbuf, wg, wu, acc_g, acc_u,
                  w_sem, out_sem, ex_send, ex_recv, ring_send, ring_recv):
    width = tok_ref.shape[1]
    block = owners * CAP
    half = n // 2
    me, e = lax.axis_index("dp"), lax.axis_index("expert")

    odd = me % 2
    pos = (1 - odd) * (me // 2) + odd * (n - 1 - me // 2)

    def at(p):
        late = p // half
        return (1 - late) * (2 * p) + late * (2 * (n - 1 - p) + 1)

    near = (at((pos + 1) % n), at((pos + n - 1) % n))

    barrier = pltpu.get_barrier_semaphore()
    for k in range(1, owners):
        pl.semaphore_signal(barrier, inc=1, device_id=(me, peer(e, k, owners)), device_id_type=MESH)
    for other in near:
        pl.semaphore_signal(barrier, inc=1, device_id=(other, e), device_id_type=MESH)

    loads = [
        pltpu.make_async_copy(gate_ref, wg, w_sem.at[0]),
        pltpu.make_async_copy(up_ref, wu, w_sem.at[1]),
    ]
    for load in loads:
        load.start()

    step_cols = 1024 if width % 1024 == 0 else 128

    def dispatch(j, carry):
        cols = pl.ds(pl.multiple_of(j * step_cols, step_cols), step_cols)
        rows = jnp.dot(hot_ref[...], tok_ref[:, cols], preferred_element_type=jnp.float32)
        rows = rows.astype(jnp.bfloat16)
        xbuf[0:CAP, cols] = rows[0:CAP]
        sbuf[:, cols] = rows[CAP:]
        return carry

    lax.fori_loop(0, width // step_cols, dispatch, 0)
    pl.semaphore_wait(barrier, owners + 1)

    pending = []
    arrive = {}
    for k in range(1, owners):
        copy = pltpu.make_async_remote_copy(
            src_ref=sbuf.at[pl.ds((k - 1) * CAP, CAP)],
            dst_ref=xbuf.at[pl.ds(k * CAP, CAP)],
            send_sem=ex_send.at[k],
            recv_sem=ex_recv.at[k],
            device_id=(me, peer(e, k, owners)),
            device_id_type=MESH,
        )
        copy.start()
        pending.append(copy)
        arrive[(0, 0, k)] = copy

    def slot(d, s):
        if s == 0:
            return 0
        return n - 1 if s == half else 2 * s - 1 + d

    def forward(d, s, c):
        copy = pltpu.make_async_remote_copy(
            src_ref=xbuf.at[pl.ds(slot(d, s - 1) * block + c * CAP, CAP)],
            dst_ref=xbuf.at[pl.ds(slot(d, s) * block + c * CAP, CAP)],
            send_sem=ring_send.at[d, s, c],
            recv_sem=ring_recv.at[d, s, c],
            device_id=(near[d], e),
            device_id_type=MESH,
        )
        copy.start()
        pending.append(copy)
        arrive[(d, s, c)] = copy

    def hidden(first, count, places):
        rows = count * block
        base = first * block
        acc_g[0:rows, :] = jnp.zeros((rows, acc_g.shape[1]), jnp.float32)
        acc_u[0:rows, :] = jnp.zeros((rows, acc_u.shape[1]), jnp.float32)

        def body(j, carry):
            cols = pl.ds(pl.multiple_of(j * step_cols, step_cols), step_cols)
            part = xbuf[base:base + rows, cols]
            dims = (((1,), (1,)), ((), ()))
            acc_g[0:rows, :] += lax.dot_general(part, wg[:, cols], dims, preferred_element_type=jnp.float32)
            acc_u[0:rows, :] += lax.dot_general(part, wu[:, cols], dims, preferred_element_type=jnp.float32)
            return carry

        lax.fori_loop(0, width // step_cols, body, 0)
        gate = acc_g[0:rows, :]
        out = (gate / (1.0 + jnp.exp(-gate)) * acc_u[0:rows, :]).astype(jnp.bfloat16)
        for i, place in enumerate(places):
            hid_ref[pl.ds(pl.multiple_of(place * block, block), block), :] = out[i * block:(i + 1) * block]

    stores = []

    def keep(first, count):
        rows = pl.ds(first * block, count * block)
        copy = pltpu.make_async_copy(xbuf.at[rows], x_ref.at[rows], out_sem.at[first])
        copy.start()
        stores.append(copy)

    for s in range(1, half + 1):
        for c in range(owners):
            if s == 1:
                if c > 0:
                    arrive[(0, 0, c)].wait_recv()
            else:
                arrive[(0, s - 1, c)].wait_recv()
                arrive[(1, s - 1, c)].wait_recv()
            if s < half:
                forward(0, s, c)
                forward(1, s, c)
            else:
                forward(0 if c < owners // 2 else 1, s, c)
        if s == 1:
            keep(0, 1)
            for load in loads:
                load.wait()
            hidden(0, 1, [pos])
        else:
            first = slot(0, s - 1)
            keep(first, 2)
            hidden(first, 2, [(pos + n - (s - 1)) % n, (pos + s - 1) % n])
    for c in range(owners):
        arrive[(0 if c < owners // 2 else 1, half, c)].wait_recv()
    keep(n - 1, 1)
    hidden(n - 1, 1, [(pos + half) % n])
    for copy in pending:
        copy.wait_send()
    for copy in stores:
        copy.wait()


def gather(hot, tokens, gate_rows, up_rows, n, owners):
    width = tokens.shape[1]
    units = gate_rows.shape[0]
    block = owners * CAP
    half = n // 2
    vmem = pl.BlockSpec(memory_space=pltpu.VMEM)
    hbm = pl.BlockSpec(memory_space=pl.ANY)
    rows = n * block
    return pl.pallas_call(
        functools.partial(gather_kernel, n, owners),
        out_shape=(
            jax.ShapeDtypeStruct((rows, width), jnp.bfloat16),
            jax.ShapeDtypeStruct((rows, units), jnp.bfloat16),
        ),
        in_specs=[vmem, vmem, hbm, hbm],
        out_specs=(hbm, vmem),
        scratch_shapes=[
            pltpu.VMEM((rows, width), jnp.bfloat16),
            pltpu.VMEM((block - CAP, width), jnp.bfloat16),
            pltpu.VMEM((units, width), jnp.bfloat16),
            pltpu.VMEM((units, width), jnp.bfloat16),
            pltpu.VMEM((2 * block, units), jnp.float32),
            pltpu.VMEM((2 * block, units), jnp.float32),
            pltpu.SemaphoreType.DMA((2,)),
            pltpu.SemaphoreType.DMA((n,)),
            pltpu.SemaphoreType.DMA((owners,)),
            pltpu.SemaphoreType.DMA((owners,)),
            pltpu.SemaphoreType.DMA((2, half + 1, owners)),
            pltpu.SemaphoreType.DMA((2, half + 1, owners)),
        ],
        compiler_params=pltpu.CompilerParams(
            collective_id=0, has_side_effects=True, vmem_limit_bytes=56 * 1024 * 1024
        ),
        cost_estimate=pl.CostEstimate(
            flops=4 * rows * width * units, bytes_accessed=6 * rows * width, transcendentals=rows * units
        ),
    )(hot, tokens, gate_rows, up_rows)


def local(tokens, routes, slot_ids, gate_weight, up_weight):
    width = tokens.shape[1]
    owners = lax.axis_size("expert")
    data_count = lax.axis_size("dp")
    e = lax.axis_index("expert")
    expert_ids = jnp.arange(owners, dtype=jnp.int32)
    member = jnp.any(routes[:, :, None] == expert_ids[None, None, :], axis=1)
    local_counts = jnp.sum(member.astype(jnp.float32), axis=0)
    totals = lax.psum(local_counts, ("dp", "expert"))
    routed = jnp.take(totals, e)
    factor = 2.0 / routed

    lanes = jnp.arange(owners * CAP, dtype=jnp.int32)
    wanted = peer(e, lanes // CAP, owners)
    matched = (routes[None, :, :] == wanted[:, None, None]) & (
        slot_ids[None, :, :] == (lanes % CAP)[:, None, None]
    )
    one_hot = jnp.any(matched, axis=2).astype(jnp.bfloat16)
    rows, hidden = gather(one_hot, tokens, gate_weight[0], up_weight[0], data_count, owners)
    col_count = width // data_count
    first_col = lax.axis_index("dp") * col_count
    hidden_all = lax.all_gather(hidden, "dp", axis=0, tiled=False)
    columns = lax.dynamic_slice_in_dim(rows, first_col, col_count, 1)
    gram = lax.dot_general(
        columns, rows, (((0,), (0,)), ((), ())), preferred_element_type=jnp.float32
    )
    down = lax.dot_general(
        hidden, hidden_all, (((0,), (1,)), ((), ())), preferred_element_type=jnp.float32
    )
    down = down.reshape(down.shape[0], -1)
    return ((gram * factor)[None], (down * factor)[None])


def solution(mesh):
    in_specs = (
        P(("dp", "expert"), None),
        P(("dp", "expert"), None),
        P(("dp", "expert"), None),
        P("expert", "dp", None),
        P("expert", "dp", None),
    )
    out_specs = (P("expert", "dp", None), P("expert", "dp", None))
    return jax.shard_map(local, mesh=mesh, in_specs=in_specs, out_specs=out_specs, check_vma=False)
```

```python
import functools

import jax
import jax.numpy as jnp
from jax import lax
from jax.experimental import pallas as pl
from jax.experimental.pallas import tpu as pltpu
from jax.sharding import PartitionSpec as P

CAP = 16
MESH = pl.DeviceIdType.MESH


def peer(e, k, owners):
    return ((e // 2 + k // 2) % (owners // 2)) * 2 + (e + k) % 2


def gather_kernel(n, owners, route_ref, slot_ref, tok_ref, gate_ref, up_ref, x_ref, down_ref, factor_ref,
                  xbuf, sbuf, wg, wu, acc_g, acc_u, hbuf, mine, counts, held_counts,
                  w_sem, out_sem, ex_send, ex_recv, cx_send, cx_recv,
                  ring_send, ring_recv, hid_send, hid_recv, cnt_send, cnt_recv):
    width = tok_ref.shape[1]
    block = owners * CAP
    half = n // 2
    me, e = lax.axis_index("dp"), lax.axis_index("expert")

    odd = me % 2
    pos = (1 - odd) * (me // 2) + odd * (n - 1 - me // 2)

    def at(p):
        late = p // half
        return (1 - late) * (2 * p) + late * (2 * (n - 1 - p) + 1)

    near = (at((pos + 1) % n), at((pos + n - 1) % n))

    barrier = pltpu.get_barrier_semaphore()
    for k in range(1, owners):
        pl.semaphore_signal(barrier, inc=1, device_id=(me, peer(e, k, owners)), device_id_type=MESH)
    for other in near:
        pl.semaphore_signal(barrier, inc=1, device_id=(other, e), device_id_type=MESH)

    loads = [
        pltpu.make_async_copy(gate_ref, wg, w_sem.at[0]),
        pltpu.make_async_copy(up_ref, wu, w_sem.at[1]),
    ]
    for load in loads:
        load.start()

    slot_rows = lax.broadcasted_iota(jnp.int32, (CAP, tok_ref.shape[0]), 0)
    picks = []
    for k in range(owners):
        wanted = peer(e, k, owners)
        pick = jnp.zeros(slot_rows.shape, jnp.float32)
        for i in range(route_ref.shape[0]):
            hit = (route_ref[i:i + 1, :] == wanted) & (slot_ref[i:i + 1, :] == slot_rows)
            pick = jnp.where(hit, 1.0, pick)
        picks.append(pick)
        counts[k] = jnp.broadcast_to(jnp.sum(pick, axis=(0, 1), keepdims=True), counts.shape[1:])
    hot = jnp.concatenate(picks, axis=0).astype(jnp.bfloat16)

    step_cols = 1024 if width % 1024 == 0 else 128

    def dispatch(j, carry):
        cols = pl.ds(pl.multiple_of(j * step_cols, step_cols), step_cols)
        rows = jnp.dot(hot, tok_ref[:, cols], preferred_element_type=jnp.float32)
        rows = rows.astype(jnp.bfloat16)
        xbuf[0:CAP, cols] = rows[0:CAP]
        sbuf[:, cols] = rows[CAP:]
        return carry

    lax.fori_loop(0, width // step_cols, dispatch, 0)
    pl.semaphore_wait(barrier, owners + 1)

    pending = []
    arrive = {}

    def send(key, src, dst, send_sem, recv_sem, target):
        copy = pltpu.make_async_remote_copy(
            src_ref=src, dst_ref=dst, send_sem=send_sem, recv_sem=recv_sem,
            device_id=target, device_id_type=MESH,
        )
        copy.start()
        pending.append(copy)
        arrive[key] = copy

    for k in range(1, owners):
        other = (me, peer(e, k, owners))
        send(("x", 0, 0, k), sbuf.at[pl.ds((k - 1) * CAP, CAP)], xbuf.at[pl.ds(k * CAP, CAP)],
             ex_send.at[k], ex_recv.at[k], other)
    for k in range(1, owners):
        other = (me, peer(e, k, owners))
        send(("c", 0, k), counts.at[k], held_counts.at[k], cx_send.at[k], cx_recv.at[k], other)

    def slot(d, s):
        if s == 0:
            return 0
        return n - 1 if s == half else 2 * s - 1 + d

    offsets = [0] * n
    for s in range(1, half):
        offsets[slot(0, s)] = n - s
        offsets[slot(1, s)] = s
    offsets[n - 1] = half
    slot_of = [offsets.index(o) for o in range(n)]

    def forward(d, s, c):
        send(("x", d, s, c),
             xbuf.at[pl.ds(slot(d, s - 1) * block + c * CAP, CAP)],
             xbuf.at[pl.ds(slot(d, s) * block + c * CAP, CAP)],
             ring_send.at[d, s, c], ring_recv.at[d, s, c], (near[d], e))

    ends = sorted({max(1, half * (i + 1) // 4) for i in range(4)})
    bounds = [0] + [n if s == half else 2 * s + 1 for s in ends]
    groups = len(bounds) - 1

    def forward_hidden(d, s, g):
        rows = pl.ds(bounds[g] * block, (bounds[g + 1] - bounds[g]) * block)
        send(("h", d, s, g), hbuf.at[slot(d, s - 1), rows], hbuf.at[slot(d, s), rows],
             hid_send.at[d, s, g], hid_recv.at[d, s, g], (near[d], e))

    def ways(s, g):
        return (0, 1) if s < half else (g % 2,)

    def forward_counts(d, s):
        send(("n", d, s), counts.at[owners + slot(d, s - 1)], counts.at[owners + slot(d, s)],
             cnt_send.at[d, s], cnt_recv.at[d, s], (near[d], e))

    def hidden(first, count):
        rows = count * block
        base = first * block
        acc_g[0:rows, :] = jnp.zeros((rows, acc_g.shape[1]), jnp.float32)
        acc_u[0:rows, :] = jnp.zeros((rows, acc_u.shape[1]), jnp.float32)

        def body(j, carry):
            cols = pl.ds(pl.multiple_of(j * step_cols, step_cols), step_cols)
            part = xbuf[base:base + rows, cols]
            dims = (((1,), (1,)), ((), ()))
            acc_g[0:rows, :] += lax.dot_general(part, wg[:, cols], dims, preferred_element_type=jnp.float32)
            acc_u[0:rows, :] += lax.dot_general(part, wu[:, cols], dims, preferred_element_type=jnp.float32)
            return carry

        lax.fori_loop(0, width // step_cols, body, 0)
        gate = acc_g[0:rows, :]
        out = (gate / (1.0 + jnp.exp(-gate)) * acc_u[0:rows, :]).astype(jnp.bfloat16)
        hbuf[0, base:base + rows, :] = out

    def down(d, s):
        j = slot(d, s)
        for r in range(n):
            own = slot_of[(offsets[j] + offsets[r]) % n]
            mine[r * block:(r + 1) * block, :] = hbuf[0, own * block:(own + 1) * block, :]
        down_ref[at((pos + offsets[j]) % n)] = lax.dot_general(
            mine[...], hbuf[j], (((0,), (0,)), ((), ())), preferred_element_type=jnp.float32
        )

    stores = []

    def keep(first, count):
        rows = pl.ds(first * block, count * block)
        copy = pltpu.make_async_copy(xbuf.at[rows], x_ref.at[rows], out_sem.at[first])
        copy.start()
        stores.append(copy)

    for s in range(1, half + 1):
        for c in range(owners):
            if s == 1:
                if c > 0:
                    arrive[("x", 0, 0, c)].wait_recv()
            else:
                arrive[("x", 0, s - 1, c)].wait_recv()
                arrive[("x", 1, s - 1, c)].wait_recv()
            if s < half:
                forward(0, s, c)
                forward(1, s, c)
            else:
                forward(0 if c < owners // 2 else 1, s, c)
        if s == 1:
            total = counts[0]
            for k in range(1, owners):
                arrive[("c", 0, k)].wait_recv()
                total = total + held_counts[k]
            counts[owners] = total
            forward_counts(0, 1)
            forward_counts(1, 1)
            keep(0, 1)
            for load in loads:
                load.wait()
            hidden(0, 1)
        else:
            arrive[("n", 0, s - 1)].wait_recv()
            arrive[("n", 1, s - 1)].wait_recv()
            forward_counts(0, s)
            if s < half:
                forward_counts(1, s)
            if s == half:
                for g in range(groups - 2):
                    forward_hidden(0, 1, g)
                    forward_hidden(1, 1, g)
            first = slot(0, s - 1)
            keep(first, 2)
            hidden(first, 2)
    if groups > 1:
        forward_hidden(0, 1, groups - 2)
        forward_hidden(1, 1, groups - 2)
    for c in range(owners):
        arrive[("x", 0 if c < owners // 2 else 1, half, c)].wait_recv()
    keep(n - 1, 1)

    def pass_on(s, g):
        for d in ways(s, g):
            arrive[("h", d, s, g)].wait_recv()
        if s < half:
            for d in ways(s + 1, g):
                forward_hidden(d, s + 1, g)

    for g in range(groups - 2):
        pass_on(1, g)
    hidden(n - 1, 1)
    forward_hidden(0, 1, groups - 1)
    forward_hidden(1, 1, groups - 1)
    down(0, 0)
    arrive[("n", 0, half)].wait_recv()
    total = counts[owners]
    for j in range(1, n):
        total = total + counts[owners + j]
    factor_ref[...] = 2.0 / total
    for s in range(1, half + 1):
        for g in range(groups):
            if s > 1 or g >= groups - 2:
                pass_on(s, g)
        down(0, s)
        if s < half:
            down(1, s)
    for copy in pending:
        copy.wait_send()
    for copy in stores:
        copy.wait()


def gather(routes_t, slots_t, tokens, gate_rows, up_rows, n, owners):
    width = tokens.shape[1]
    units = gate_rows.shape[0]
    block = owners * CAP
    half = n // 2
    vmem = pl.BlockSpec(memory_space=pltpu.VMEM)
    hbm = pl.BlockSpec(memory_space=pl.ANY)
    rows = n * block
    dma = pltpu.SemaphoreType.DMA
    return pl.pallas_call(
        functools.partial(gather_kernel, n, owners),
        out_shape=(
            jax.ShapeDtypeStruct((rows, width), jnp.bfloat16),
            jax.ShapeDtypeStruct((n, units, units), jnp.float32),
            jax.ShapeDtypeStruct((8, 128), jnp.float32),
        ),
        in_specs=[vmem, vmem, vmem, hbm, hbm],
        out_specs=(hbm, vmem, vmem),
        scratch_shapes=[
            pltpu.VMEM((rows, width), jnp.bfloat16),
            pltpu.VMEM((block - CAP, width), jnp.bfloat16),
            pltpu.VMEM((units, width), jnp.bfloat16),
            pltpu.VMEM((units, width), jnp.bfloat16),
            pltpu.VMEM((2 * block, units), jnp.float32),
            pltpu.VMEM((2 * block, units), jnp.float32),
            pltpu.VMEM((n, rows, units), jnp.bfloat16),
            pltpu.VMEM((rows, units), jnp.bfloat16),
            pltpu.VMEM((owners + n, 8, 128), jnp.float32),
            pltpu.VMEM((owners, 8, 128), jnp.float32),
            dma((2,)),
            dma((n,)),
            dma((owners,)),
            dma((owners,)),
            dma((owners,)),
            dma((owners,)),
            dma((2, half + 1, owners)),
            dma((2, half + 1, owners)),
            dma((2, half + 1, 4)),
            dma((2, half + 1, 4)),
            dma((2, half + 1)),
            dma((2, half + 1)),
        ],
        compiler_params=pltpu.CompilerParams(
            collective_id=0, has_side_effects=True, vmem_limit_bytes=60 * 1024 * 1024
        ),
        cost_estimate=pl.CostEstimate(
            flops=4 * rows * width * units, bytes_accessed=6 * rows * width, transcendentals=rows * units
        ),
    )(routes_t, slots_t, tokens, gate_rows, up_rows)


def gram_kernel(place_ref, cols_ref, rows_ref, factor_ref, out_ref, turned):
    @pl.when(pl.program_id(0) == 0)
    def _():
        turned[...] = cols_ref[...].T

    out_ref[...] = factor_ref[0:1, 0:1] * jnp.dot(
        turned[...], rows_ref[...], preferred_element_type=jnp.float32
    )


def gram(rows, factor, place, col_count):
    depth, width = rows.shape
    tile = 512 if width % 512 == 0 else 128
    if col_count % 128 == 0:
        columns = rows
        spec = pl.BlockSpec((depth, col_count), lambda j, p: (0, p[0]))
    else:
        columns = lax.dynamic_slice_in_dim(rows, place * col_count, col_count, 1)
        spec = pl.BlockSpec((depth, col_count), lambda j, p: (0, 0))
    return pl.pallas_call(
        gram_kernel,
        out_shape=jax.ShapeDtypeStruct((col_count, width), jnp.float32),
        grid_spec=pltpu.PrefetchScalarGridSpec(
            num_scalar_prefetch=1,
            grid=(width // tile,),
            in_specs=[
                spec,
                pl.BlockSpec((depth, tile), lambda j, p: (0, j)),
                pl.BlockSpec((8, 128), lambda j, p: (0, 0)),
            ],
            out_specs=pl.BlockSpec((col_count, tile), lambda j, p: (0, j)),
            scratch_shapes=[pltpu.VMEM((col_count, depth), jnp.bfloat16)],
        ),
        compiler_params=pltpu.CompilerParams(vmem_limit_bytes=48 * 1024 * 1024),
        cost_estimate=pl.CostEstimate(
            flops=2 * depth * col_count * width, bytes_accessed=4 * col_count * width, transcendentals=0
        ),
    )(place.reshape(1), columns, rows, factor)


def local(tokens, routes, slot_ids, gate_weight, up_weight):
    width = tokens.shape[1]
    owners = lax.axis_size("expert")
    data_count = lax.axis_size("dp")
    rows, down, factor = gather(
        routes.T, slot_ids.T, tokens, gate_weight[0], up_weight[0], data_count, owners
    )
    place = lax.axis_index("dp").astype(jnp.int32)
    input_block = gram(rows, factor, place, width // data_count)
    down = jnp.transpose(down, (1, 0, 2)).reshape(down.shape[1], -1) * factor[0, 0]
    return (input_block[None], down[None])


def solution(mesh):
    in_specs = (
        P(("dp", "expert"), None),
        P(("dp", "expert"), None),
        P(("dp", "expert"), None),
        P("expert", "dp", None),
        P("expert", "dp", None),
    )
    out_specs = (P("expert", "dp", None), P("expert", "dp", None))
    return jax.shard_map(local, mesh=mesh, in_specs=in_specs, out_specs=out_specs, check_vma=False)
```

```python
import functools

import jax
import jax.numpy as jnp
from jax import lax
from jax.experimental import pallas as pl
from jax.experimental.pallas import tpu as pltpu
from jax.sharding import PartitionSpec as P

CAP = 16
MESH = pl.DeviceIdType.MESH


def peer(e, k, owners):
    return ((e // 2 + k // 2) % (owners // 2)) * 2 + (e + k) % 2


def gather_kernel(n, owners, route_ref, slot_ref, tok_ref, gate_ref, up_ref,
                  x_ref, down_ref, factor_ref, turned_ref,
                  xbuf, sbuf, wg, wu, acc_g, acc_u, hbuf, mine, counts, held_counts,
                  w_sem, out_sem, ex_send, ex_recv, cx_send, cx_recv,
                  ring_send, ring_recv, hid_send, hid_recv, cnt_send, cnt_recv):
    width = tok_ref.shape[1]
    block = owners * CAP
    half = n // 2
    me, e = lax.axis_index("dp"), lax.axis_index("expert")

    odd = me % 2
    pos = (1 - odd) * (me // 2) + odd * (n - 1 - me // 2)

    def at(p):
        late = p // half
        return (1 - late) * (2 * p) + late * (2 * (n - 1 - p) + 1)

    near = (at((pos + 1) % n), at((pos + n - 1) % n))

    barrier = pltpu.get_barrier_semaphore()
    for k in range(1, owners):
        pl.semaphore_signal(barrier, inc=1, device_id=(me, peer(e, k, owners)), device_id_type=MESH)
    for other in near:
        pl.semaphore_signal(barrier, inc=1, device_id=(other, e), device_id_type=MESH)

    loads = [
        pltpu.make_async_copy(gate_ref, wg, w_sem.at[0]),
        pltpu.make_async_copy(up_ref, wu, w_sem.at[1]),
    ]
    for load in loads:
        load.start()

    slot_rows = lax.broadcasted_iota(jnp.int32, (CAP, tok_ref.shape[0]), 0)
    picks = []
    for k in range(owners):
        wanted = peer(e, k, owners)
        pick = jnp.zeros(slot_rows.shape, jnp.float32)
        for i in range(route_ref.shape[0]):
            hit = (route_ref[i:i + 1, :] == wanted) & (slot_ref[i:i + 1, :] == slot_rows)
            pick = jnp.where(hit, 1.0, pick)
        picks.append(pick)
        counts[k] = jnp.broadcast_to(jnp.sum(pick, axis=(0, 1), keepdims=True), counts.shape[1:])
    hot = jnp.concatenate(picks, axis=0).astype(jnp.bfloat16)

    step_cols = 1024 if width % 1024 == 0 else 128

    def dispatch(j, carry):
        cols = pl.ds(pl.multiple_of(j * step_cols, step_cols), step_cols)
        rows = jnp.dot(hot, tok_ref[:, cols], preferred_element_type=jnp.float32)
        rows = rows.astype(jnp.bfloat16)
        xbuf[0:CAP, cols] = rows[0:CAP]
        sbuf[:, cols] = rows[CAP:]
        return carry

    lax.fori_loop(0, width // step_cols, dispatch, 0)
    pl.semaphore_wait(barrier, owners + 1)

    pending = []
    arrive = {}

    def send(key, src, dst, send_sem, recv_sem, target):
        copy = pltpu.make_async_remote_copy(
            src_ref=src, dst_ref=dst, send_sem=send_sem, recv_sem=recv_sem,
            device_id=target, device_id_type=MESH,
        )
        copy.start()
        pending.append(copy)
        arrive[key] = copy

    for k in range(1, owners):
        other = (me, peer(e, k, owners))
        send(("x", 0, 0, k), sbuf.at[pl.ds((k - 1) * CAP, CAP)], xbuf.at[pl.ds(k * CAP, CAP)],
             ex_send.at[k], ex_recv.at[k], other)
    for k in range(1, owners):
        other = (me, peer(e, k, owners))
        send(("c", 0, k), counts.at[k], held_counts.at[k], cx_send.at[k], cx_recv.at[k], other)

    def slot(d, s):
        if s == 0:
            return 0
        return n - 1 if s == half else 2 * s - 1 + d

    offsets = [0] * n
    for s in range(1, half):
        offsets[slot(0, s)] = n - s
        offsets[slot(1, s)] = s
    offsets[n - 1] = half
    slot_of = [offsets.index(o) for o in range(n)]

    def forward(d, s, c):
        send(("x", d, s, c),
             xbuf.at[pl.ds(slot(d, s - 1) * block + c * CAP, CAP)],
             xbuf.at[pl.ds(slot(d, s) * block + c * CAP, CAP)],
             ring_send.at[d, s, c], ring_recv.at[d, s, c], (near[d], e))

    ends = sorted({max(1, half * (i + 1) // 4) for i in range(4)})
    bounds = [0] + [n if s == half else 2 * s + 1 for s in ends]
    groups = len(bounds) - 1

    def forward_hidden(d, s, g):
        rows = pl.ds(bounds[g] * block, (bounds[g + 1] - bounds[g]) * block)
        send(("h", d, s, g), hbuf.at[slot(d, s - 1), rows], hbuf.at[slot(d, s), rows],
             hid_send.at[d, s, g], hid_recv.at[d, s, g], (near[d], e))

    def ways(s, g):
        return (0, 1) if s < half else (g % 2,)

    def forward_counts(d, s):
        send(("n", d, s), counts.at[owners + slot(d, s - 1)], counts.at[owners + slot(d, s)],
             cnt_send.at[d, s], cnt_recv.at[d, s], (near[d], e))

    def hidden(first, count):
        rows = count * block
        base = first * block
        acc_g[0:rows, :] = jnp.zeros((rows, acc_g.shape[1]), jnp.float32)
        acc_u[0:rows, :] = jnp.zeros((rows, acc_u.shape[1]), jnp.float32)

        def body(j, carry):
            cols = pl.ds(pl.multiple_of(j * step_cols, step_cols), step_cols)
            part = xbuf[base:base + rows, cols]
            dims = (((1,), (1,)), ((), ()))
            acc_g[0:rows, :] += lax.dot_general(part, wg[:, cols], dims, preferred_element_type=jnp.float32)
            acc_u[0:rows, :] += lax.dot_general(part, wu[:, cols], dims, preferred_element_type=jnp.float32)
            return carry

        lax.fori_loop(0, width // step_cols, body, 0)
        gate = acc_g[0:rows, :]
        out = (gate / (1.0 + jnp.exp(-gate)) * acc_u[0:rows, :]).astype(jnp.bfloat16)
        hbuf[0, base:base + rows, :] = out

    def down(d, s):
        j = slot(d, s)
        for r in range(n):
            own = slot_of[(offsets[j] + offsets[r]) % n]
            mine[r * block:(r + 1) * block, :] = hbuf[0, own * block:(own + 1) * block, :]
        part = factor_ref[0:1, 0:1] * lax.dot_general(
            mine[...], hbuf[j], (((0,), (0,)), ((), ())), preferred_element_type=jnp.float32
        )
        place = at((pos + offsets[j]) % n)
        if len(down_ref.shape) == 2:
            units = down_ref.shape[0]
            down_ref[:, pl.ds(pl.multiple_of(place * units, units), units)] = part
        else:
            down_ref[place] = part

    stores = []

    def keep(first, count):
        rows = pl.ds(first * block, count * block)
        copy = pltpu.make_async_copy(xbuf.at[rows], x_ref.at[rows], out_sem.at[first])
        copy.start()
        stores.append(copy)

    for s in range(1, half + 1):
        for c in range(owners):
            if s == 1:
                if c > 0:
                    arrive[("x", 0, 0, c)].wait_recv()
            else:
                arrive[("x", 0, s - 1, c)].wait_recv()
                arrive[("x", 1, s - 1, c)].wait_recv()
            if s < half:
                forward(0, s, c)
                forward(1, s, c)
            else:
                forward(0 if c < owners // 2 else 1, s, c)
        if s == 1:
            total = counts[0]
            for k in range(1, owners):
                arrive[("c", 0, k)].wait_recv()
                total = total + held_counts[k]
            counts[owners] = total
            forward_counts(0, 1)
            forward_counts(1, 1)
            keep(0, 1)
            for load in loads:
                load.wait()
            hidden(0, 1)
        else:
            arrive[("n", 0, s - 1)].wait_recv()
            arrive[("n", 1, s - 1)].wait_recv()
            forward_counts(0, s)
            if s < half:
                forward_counts(1, s)
            if s == half:
                for g in range(groups - 2):
                    forward_hidden(0, 1, g)
                    forward_hidden(1, 1, g)
            first = slot(0, s - 1)
            keep(first, 2)
            hidden(first, 2)
    if groups > 1:
        forward_hidden(0, 1, groups - 2)
        forward_hidden(1, 1, groups - 2)
    for c in range(owners):
        arrive[("x", 0 if c < owners // 2 else 1, half, c)].wait_recv()
    keep(n - 1, 1)

    def pass_on(s, g):
        for d in ways(s, g):
            arrive[("h", d, s, g)].wait_recv()
        if s < half:
            for d in ways(s + 1, g):
                forward_hidden(d, s + 1, g)

    for g in range(groups - 2):
        pass_on(1, g)
    hidden(n - 1, 1)
    forward_hidden(0, 1, groups - 1)
    forward_hidden(1, 1, groups - 1)
    arrive[("n", 0, half)].wait_recv()
    total = counts[owners]
    for j in range(1, n):
        total = total + counts[owners + j]
    factor_ref[...] = 2.0 / total
    down(0, 0)
    for s in range(1, half + 1):
        for g in range(groups):
            if s > 1 or g >= groups - 2:
                pass_on(s, g)
        if s == 2:
            count = turned_ref.shape[0]
            if count == width // n:
                turned_ref[...] = xbuf[:, pl.ds(pl.multiple_of(me * count, 128), count)].T
            else:
                turned_ref[...] = jnp.zeros(turned_ref.shape, jnp.bfloat16)
        down(0, s)
        if s < half:
            down(1, s)
    for copy in pending:
        copy.wait_send()
    for copy in stores:
        copy.wait()


def gather(routes_t, slots_t, tokens, gate_rows, up_rows, n, owners):
    width = tokens.shape[1]
    units = gate_rows.shape[0]
    block = owners * CAP
    half = n // 2
    vmem = pl.BlockSpec(memory_space=pltpu.VMEM)
    hbm = pl.BlockSpec(memory_space=pl.ANY)
    rows = n * block
    dma = pltpu.SemaphoreType.DMA
    return pl.pallas_call(
        functools.partial(gather_kernel, n, owners),
        out_shape=(
            jax.ShapeDtypeStruct((rows, width), jnp.bfloat16),
            jax.ShapeDtypeStruct((units, n * units) if units % 128 == 0 else (n, units, units), jnp.float32),
            jax.ShapeDtypeStruct((8, 128), jnp.float32),
            jax.ShapeDtypeStruct((width // n, rows) if (width // n) % 128 == 0 else (8, 128), jnp.bfloat16),
        ),
        in_specs=[vmem, vmem, vmem, hbm, hbm],
        out_specs=(hbm, vmem, vmem, vmem),
        scratch_shapes=[
            pltpu.VMEM((rows, width), jnp.bfloat16),
            pltpu.VMEM((block - CAP, width), jnp.bfloat16),
            pltpu.VMEM((units, width), jnp.bfloat16),
            pltpu.VMEM((units, width), jnp.bfloat16),
            pltpu.VMEM((2 * block, units), jnp.float32),
            pltpu.VMEM((2 * block, units), jnp.float32),
            pltpu.VMEM((n, rows, units), jnp.bfloat16),
            pltpu.VMEM((rows, units), jnp.bfloat16),
            pltpu.VMEM((owners + n, 8, 128), jnp.float32),
            pltpu.VMEM((owners, 8, 128), jnp.float32),
            dma((2,)),
            dma((n,)),
            dma((owners,)),
            dma((owners,)),
            dma((owners,)),
            dma((owners,)),
            dma((2, half + 1, owners)),
            dma((2, half + 1, owners)),
            dma((2, half + 1, 4)),
            dma((2, half + 1, 4)),
            dma((2, half + 1)),
            dma((2, half + 1)),
        ],
        compiler_params=pltpu.CompilerParams(
            collective_id=0, has_side_effects=True, vmem_limit_bytes=60 * 1024 * 1024
        ),
        cost_estimate=pl.CostEstimate(
            flops=4 * rows * width * units, bytes_accessed=6 * rows * width, transcendentals=rows * units
        ),
    )(routes_t, slots_t, tokens, gate_rows, up_rows)


def gram_kernel(tile, pieces, turned_ref, rows_ref, factor_ref, down_in, out_ref, down_out,
                held, parts, in_sem, out_sem, down_sem):
    width = rows_ref.shape[1]
    slots, count = parts.shape[0], parts.shape[1]
    steps = width // tile
    piece = count // pieces

    def load(j):
        cols = pl.ds(pl.multiple_of(j * tile, tile), tile)
        return pltpu.make_async_copy(rows_ref.at[:, cols], held.at[:, cols], in_sem.at[j])

    def store(j, i):
        b = j % slots
        rows = pl.ds(i * piece, piece)
        cols = pl.ds(pl.multiple_of(j * tile, tile), tile)
        return pltpu.make_async_copy(parts.at[b, rows], out_ref.at[rows, cols], out_sem.at[b, i])

    for j in range(steps):
        load(j).start()
    down_copy = pltpu.make_async_copy(down_in, down_out, down_sem.at[0])
    down_copy.start()

    def body(j, carry):
        load(j).wait()

        @pl.when(j >= slots)
        def _():
            for i in range(pieces):
                store(j - slots, i).wait()

        cols = pl.ds(pl.multiple_of(j * tile, tile), tile)
        for i in range(pieces):
            rows = slice(i * piece, (i + 1) * piece)
            parts[j % slots, rows] = factor_ref[0:1, 0:1] * jnp.dot(
                turned_ref[rows, :], held[:, cols], preferred_element_type=jnp.float32
            )
            store(j, i).start()
        return carry

    lax.fori_loop(0, steps, body, 0)
    for j in range(max(0, steps - slots), steps):
        for i in range(pieces):
            store(j, i).wait()
    down_copy.wait()


def gram(turned, rows, factor, down):
    depth, width = rows.shape
    count = turned.shape[0]
    tile = 512 if width % 512 == 0 else 128
    pieces = 2 if count % 16 == 0 else 1
    slots = 4
    vmem = pl.BlockSpec(memory_space=pltpu.VMEM)
    hbm = pl.BlockSpec(memory_space=pl.ANY)
    dma = pltpu.SemaphoreType.DMA
    return pl.pallas_call(
        functools.partial(gram_kernel, tile, pieces),
        out_shape=(
            jax.ShapeDtypeStruct((count, width), jnp.float32),
            jax.ShapeDtypeStruct(down.shape, jnp.float32),
        ),
        in_specs=[vmem, hbm, vmem, hbm],
        out_specs=(hbm, hbm),
        scratch_shapes=[
            pltpu.VMEM((depth, width), jnp.bfloat16),
            pltpu.VMEM((slots, count, tile), jnp.float32),
            dma((width // tile,)),
            dma((slots, pieces)),
            dma((1,)),
        ],
        compiler_params=pltpu.CompilerParams(vmem_limit_bytes=60 * 1024 * 1024),
        cost_estimate=pl.CostEstimate(
            flops=2 * depth * count * width, bytes_accessed=4 * count * width, transcendentals=0
        ),
    )(turned, rows, factor, down)


def local(tokens, routes, slot_ids, gate_weight, up_weight):
    width = tokens.shape[1]
    owners = lax.axis_size("expert")
    data_count = lax.axis_size("dp")
    rows, down, factor, turned = gather(
        routes.T, slot_ids.T, tokens, gate_weight[0], up_weight[0], data_count, owners
    )
    count = width // data_count
    if turned.shape[0] != count:
        turned = lax.dynamic_slice_in_dim(rows, lax.axis_index("dp") * count, count, 1).T
    if down.ndim == 3:
        down = jnp.transpose(down, (1, 0, 2)).reshape(down.shape[1], -1)
    input_block, down_block = gram(turned, rows, factor, down)
    return (input_block[None], down_block[None])


def solution(mesh):
    in_specs = (
        P(("dp", "expert"), None),
        P(("dp", "expert"), None),
        P(("dp", "expert"), None),
        P("expert", "dp", None),
        P("expert", "dp", None),
    )
    out_specs = (P("expert", "dp", None), P("expert", "dp", None))
    return jax.shard_map(local, mesh=mesh, in_specs=in_specs, out_specs=out_specs, check_vma=False)
```

```python
import functools

import jax
import jax.numpy as jnp
from jax import lax
from jax.experimental import pallas as pl
from jax.experimental.pallas import tpu as pltpu
from jax.sharding import PartitionSpec as P

CAP = 16
MESH = pl.DeviceIdType.MESH


def peer(e, k, owners):
    return ((e // 2 + k // 2) % (owners // 2)) * 2 + (e + k) % 2


def gather_kernel(n, owners, route_ref, slot_ref, tok_ref, gate_ref, up_ref,
                  x_ref, down_ref, factor_ref, turned_ref,
                  xbuf, sbuf, tok, wg, wu, acc_g, acc_u, hbuf, mine, counts, held_counts,
                  tok_sem, w_sem, out_sem, ex_send, ex_recv, cx_send, cx_recv,
                  ring_send, ring_recv, hid_send, hid_recv, cnt_send, cnt_recv):
    width = tok_ref.shape[1]
    block = owners * CAP
    half = n // 2
    me, e = lax.axis_index("dp"), lax.axis_index("expert")

    odd = me % 2
    pos = (1 - odd) * (me // 2) + odd * (n - 1 - me // 2)

    def at(p):
        late = p // half
        return (1 - late) * (2 * p) + late * (2 * (n - 1 - p) + 1)

    near = (at((pos + 1) % n), at((pos + n - 1) % n))

    step_cols = 1024 if width % 1024 == 0 else 128

    def panel(j):
        cols = pl.ds(pl.multiple_of(j * step_cols, step_cols), step_cols)
        return pltpu.make_async_copy(tok_ref.at[:, cols], tok.at[:, cols], tok_sem.at[j])

    for j in range(width // step_cols):
        panel(j).start()

    barrier = pltpu.get_barrier_semaphore()
    for k in range(1, owners):
        pl.semaphore_signal(barrier, inc=1, device_id=(me, peer(e, k, owners)), device_id_type=MESH)
    for other in near:
        pl.semaphore_signal(barrier, inc=1, device_id=(other, e), device_id_type=MESH)

    loads = [
        pltpu.make_async_copy(gate_ref, wg, w_sem.at[0]),
        pltpu.make_async_copy(up_ref, wu, w_sem.at[1]),
    ]

    slot_rows = lax.broadcasted_iota(jnp.int32, (CAP, tok_ref.shape[0]), 0)
    picks = []
    for k in range(owners):
        wanted = peer(e, k, owners)
        pick = jnp.zeros(slot_rows.shape, jnp.float32)
        for i in range(route_ref.shape[0]):
            hit = (route_ref[i:i + 1, :] == wanted) & (slot_ref[i:i + 1, :] == slot_rows)
            pick = jnp.where(hit, 1.0, pick)
        picks.append(pick)
        counts[k] = jnp.broadcast_to(jnp.sum(pick, axis=(0, 1), keepdims=True), counts.shape[1:])
    hot = jnp.concatenate(picks, axis=0).astype(jnp.bfloat16)

    def dispatch(j, carry):
        cols = pl.ds(pl.multiple_of(j * step_cols, step_cols), step_cols)
        panel(j).wait()
        rows = jnp.dot(hot, tok[:, cols], preferred_element_type=jnp.float32)
        rows = rows.astype(jnp.bfloat16)
        xbuf[0:CAP, cols] = rows[0:CAP]
        sbuf[:, cols] = rows[CAP:]
        return carry

    lax.fori_loop(0, width // step_cols, dispatch, 0)
    pl.semaphore_wait(barrier, owners + 1)
    for load in loads:
        load.start()

    pending = []
    arrive = {}

    def send(key, src, dst, send_sem, recv_sem, target):
        copy = pltpu.make_async_remote_copy(
            src_ref=src, dst_ref=dst, send_sem=send_sem, recv_sem=recv_sem,
            device_id=target, device_id_type=MESH,
        )
        copy.start()
        pending.append(copy)
        arrive[key] = copy

    for k in range(1, owners):
        other = (me, peer(e, k, owners))
        send(("x", 0, 0, k), sbuf.at[pl.ds((k - 1) * CAP, CAP)], xbuf.at[pl.ds(k * CAP, CAP)],
             ex_send.at[k], ex_recv.at[k], other)
    for k in range(1, owners):
        other = (me, peer(e, k, owners))
        send(("c", 0, k), counts.at[k], held_counts.at[k], cx_send.at[k], cx_recv.at[k], other)

    def slot(d, s):
        if s == 0:
            return 0
        return n - 1 if s == half else 2 * s - 1 + d

    offsets = [0] * n
    for s in range(1, half):
        offsets[slot(0, s)] = n - s
        offsets[slot(1, s)] = s
    offsets[n - 1] = half
    slot_of = [offsets.index(o) for o in range(n)]

    def forward(d, s, c):
        send(("x", d, s, c),
             xbuf.at[pl.ds(slot(d, s - 1) * block + c * CAP, CAP)],
             xbuf.at[pl.ds(slot(d, s) * block + c * CAP, CAP)],
             ring_send.at[d, s, c], ring_recv.at[d, s, c], (near[d], e))

    ends = sorted({max(1, half * (i + 1) // 4) for i in range(4)})
    bounds = [0] + [n if s == half else 2 * s + 1 for s in ends]
    groups = len(bounds) - 1

    def forward_hidden(d, s, g):
        rows = pl.ds(bounds[g] * block, (bounds[g + 1] - bounds[g]) * block)
        send(("h", d, s, g), hbuf.at[slot(d, s - 1), rows], hbuf.at[slot(d, s), rows],
             hid_send.at[d, s, g], hid_recv.at[d, s, g], (near[d], e))

    def ways(s, g):
        return (0, 1) if s < half else (g % 2,)

    def forward_counts(d, s):
        send(("n", d, s), counts.at[owners + slot(d, s - 1)], counts.at[owners + slot(d, s)],
             cnt_send.at[d, s], cnt_recv.at[d, s], (near[d], e))

    def hidden(first, count):
        rows = count * block
        base = first * block
        acc_g[0:rows, :] = jnp.zeros((rows, acc_g.shape[1]), jnp.float32)
        acc_u[0:rows, :] = jnp.zeros((rows, acc_u.shape[1]), jnp.float32)

        def body(j, carry):
            cols = pl.ds(pl.multiple_of(j * step_cols, step_cols), step_cols)
            part = xbuf[base:base + rows, cols]
            dims = (((1,), (1,)), ((), ()))
            acc_g[0:rows, :] += lax.dot_general(part, wg[:, cols], dims, preferred_element_type=jnp.float32)
            acc_u[0:rows, :] += lax.dot_general(part, wu[:, cols], dims, preferred_element_type=jnp.float32)
            return carry

        lax.fori_loop(0, width // step_cols, body, 0)
        gate = acc_g[0:rows, :]
        out = (gate / (1.0 + jnp.exp(-gate)) * acc_u[0:rows, :]).astype(jnp.bfloat16)
        hbuf[0, base:base + rows, :] = out

    def down(d, s):
        j = slot(d, s)
        for r in range(n):
            own = slot_of[(offsets[j] + offsets[r]) % n]
            mine[r * block:(r + 1) * block, :] = hbuf[0, own * block:(own + 1) * block, :]
        part = factor_ref[0:1, 0:1] * lax.dot_general(
            mine[...], hbuf[j], (((0,), (0,)), ((), ())), preferred_element_type=jnp.float32
        )
        place = at((pos + offsets[j]) % n)
        if len(down_ref.shape) == 2:
            units = down_ref.shape[0]
            down_ref[:, pl.ds(pl.multiple_of(place * units, units), units)] = part
        else:
            down_ref[place] = part

    stores = []

    def keep(first, count):
        rows = pl.ds(first * block, count * block)
        copy = pltpu.make_async_copy(xbuf.at[rows], x_ref.at[rows], out_sem.at[first])
        copy.start()
        stores.append(copy)

    for s in range(1, half + 1):
        for c in range(owners):
            if s == 1:
                if c > 0:
                    arrive[("x", 0, 0, c)].wait_recv()
            else:
                arrive[("x", 0, s - 1, c)].wait_recv()
                arrive[("x", 1, s - 1, c)].wait_recv()
            if s < half:
                forward(0, s, c)
                forward(1, s, c)
            else:
                forward(0 if c < owners // 2 else 1, s, c)
        if s == 1:
            total = counts[0]
            for k in range(1, owners):
                arrive[("c", 0, k)].wait_recv()
                total = total + held_counts[k]
            counts[owners] = total
            forward_counts(0, 1)
            forward_counts(1, 1)
            keep(0, 1)
            for load in loads:
                load.wait()
            hidden(0, 1)
        else:
            arrive[("n", 0, s - 1)].wait_recv()
            arrive[("n", 1, s - 1)].wait_recv()
            forward_counts(0, s)
            if s < half:
                forward_counts(1, s)
            if s == half:
                for g in range(groups - 2):
                    forward_hidden(0, 1, g)
                    forward_hidden(1, 1, g)
            first = slot(0, s - 1)
            keep(first, 2)
            hidden(first, 2)
    if groups > 1:
        forward_hidden(0, 1, groups - 2)
        forward_hidden(1, 1, groups - 2)
    for c in range(owners):
        arrive[("x", 0 if c < owners // 2 else 1, half, c)].wait_recv()
    keep(n - 1, 1)

    def pass_on(s, g):
        for d in ways(s, g):
            arrive[("h", d, s, g)].wait_recv()
        if s < half:
            for d in ways(s + 1, g):
                forward_hidden(d, s + 1, g)

    for g in range(groups - 2):
        pass_on(1, g)
    hidden(n - 1, 1)
    forward_hidden(0, 1, groups - 1)
    forward_hidden(1, 1, groups - 1)
    arrive[("n", 0, half)].wait_recv()
    total = counts[owners]
    for j in range(1, n):
        total = total + counts[owners + j]
    factor_ref[...] = 2.0 / total
    down(0, 0)
    for s in range(1, half + 1):
        for g in range(groups):
            if s > 1 or g >= groups - 2:
                pass_on(s, g)
        if s == 2:
            count = turned_ref.shape[0]
            if count == width // n:
                turned_ref[...] = xbuf[:, pl.ds(pl.multiple_of(me * count, 128), count)].T
            else:
                turned_ref[...] = jnp.zeros(turned_ref.shape, jnp.bfloat16)
        down(0, s)
        if s < half:
            down(1, s)
    for copy in pending:
        copy.wait_send()
    for copy in stores:
        copy.wait()


def gather(routes_t, slots_t, tokens, gate_rows, up_rows, n, owners):
    width = tokens.shape[1]
    units = gate_rows.shape[0]
    block = owners * CAP
    half = n // 2
    vmem = pl.BlockSpec(memory_space=pltpu.VMEM)
    hbm = pl.BlockSpec(memory_space=pl.ANY)
    rows = n * block
    dma = pltpu.SemaphoreType.DMA
    return pl.pallas_call(
        functools.partial(gather_kernel, n, owners),
        out_shape=(
            jax.ShapeDtypeStruct((rows, width), jnp.bfloat16),
            jax.ShapeDtypeStruct((units, n * units) if units % 128 == 0 else (n, units, units), jnp.float32),
            jax.ShapeDtypeStruct((8, 128), jnp.float32),
            jax.ShapeDtypeStruct((width // n, rows) if (width // n) % 128 == 0 else (8, 128), jnp.bfloat16),
        ),
        in_specs=[vmem, vmem, hbm, hbm, hbm],
        out_specs=(hbm, vmem, vmem, vmem),
        scratch_shapes=[
            pltpu.VMEM((rows, width), jnp.bfloat16),
            pltpu.VMEM((block - CAP, width), jnp.bfloat16),
            pltpu.VMEM(tokens.shape, jnp.bfloat16),
            pltpu.VMEM((units, width), jnp.bfloat16),
            pltpu.VMEM((units, width), jnp.bfloat16),
            pltpu.VMEM((2 * block, units), jnp.float32),
            pltpu.VMEM((2 * block, units), jnp.float32),
            pltpu.VMEM((n, rows, units), jnp.bfloat16),
            pltpu.VMEM((rows, units), jnp.bfloat16),
            pltpu.VMEM((owners + n, 8, 128), jnp.float32),
            pltpu.VMEM((owners, 8, 128), jnp.float32),
            dma((width // (1024 if width % 1024 == 0 else 128),)),
            dma((2,)),
            dma((n,)),
            dma((owners,)),
            dma((owners,)),
            dma((owners,)),
            dma((owners,)),
            dma((2, half + 1, owners)),
            dma((2, half + 1, owners)),
            dma((2, half + 1, 4)),
            dma((2, half + 1, 4)),
            dma((2, half + 1)),
            dma((2, half + 1)),
        ],
        compiler_params=pltpu.CompilerParams(
            collective_id=0, has_side_effects=True, vmem_limit_bytes=60 * 1024 * 1024
        ),
        cost_estimate=pl.CostEstimate(
            flops=4 * rows * width * units, bytes_accessed=6 * rows * width, transcendentals=rows * units
        ),
    )(routes_t, slots_t, tokens, gate_rows, up_rows)


def gram_kernel(tile, pieces, turned_ref, rows_ref, factor_ref, down_in, out_ref, down_out,
                held, parts, turned, down_held, in_sem, out_sem, own_sem):
    width = rows_ref.shape[1]
    slots, count = parts.shape[0], parts.shape[1]
    steps = width // tile
    piece = count // pieces

    def load(j):
        cols = pl.ds(pl.multiple_of(j * tile, tile), tile)
        return pltpu.make_async_copy(rows_ref.at[:, cols], held.at[:, cols], in_sem.at[j])

    def store(j, i):
        b = j % slots
        rows = pl.ds(i * piece, piece)
        cols = pl.ds(pl.multiple_of(j * tile, tile), tile)
        return pltpu.make_async_copy(parts.at[b, rows], out_ref.at[rows, cols], out_sem.at[b, i])

    turned_load = pltpu.make_async_copy(turned_ref, turned, own_sem.at[0])
    down_load = pltpu.make_async_copy(down_in, down_held, own_sem.at[1])
    down_store = pltpu.make_async_copy(down_held, down_out, own_sem.at[2])
    turned_load.start()
    for j in range(steps):
        load(j).start()
    down_load.start()
    turned_load.wait()

    def body(j, carry):
        load(j).wait()

        @pl.when(j >= slots)
        def _():
            for i in range(pieces):
                store(j - slots, i).wait()

        cols = pl.ds(pl.multiple_of(j * tile, tile), tile)
        for i in range(pieces):
            rows = slice(i * piece, (i + 1) * piece)
            parts[j % slots, rows] = factor_ref[0:1, 0:1] * jnp.dot(
                turned[rows, :], held[:, cols], preferred_element_type=jnp.float32
            )
            store(j, i).start()
        return carry

    early = min(slots, steps)
    lax.fori_loop(0, early, body, 0)
    down_load.wait()
    down_store.start()
    lax.fori_loop(early, steps, body, 0)
    for j in range(max(0, steps - slots), steps):
        for i in range(pieces):
            store(j, i).wait()
    down_store.wait()


def gram(turned, rows, factor, down):
    depth, width = rows.shape
    count = turned.shape[0]
    tile = 512 if width % 512 == 0 else 128
    pieces = 2 if count % 16 == 0 else 1
    slots = 4
    vmem = pl.BlockSpec(memory_space=pltpu.VMEM)
    hbm = pl.BlockSpec(memory_space=pl.ANY)
    dma = pltpu.SemaphoreType.DMA
    return pl.pallas_call(
        functools.partial(gram_kernel, tile, pieces),
        out_shape=(
            jax.ShapeDtypeStruct((count, width), jnp.float32),
            jax.ShapeDtypeStruct(down.shape, jnp.float32),
        ),
        in_specs=[hbm, hbm, vmem, hbm],
        out_specs=(hbm, hbm),
        scratch_shapes=[
            pltpu.VMEM((depth, width), jnp.bfloat16),
            pltpu.VMEM((slots, count, tile), jnp.float32),
            pltpu.VMEM(turned.shape, jnp.bfloat16),
            pltpu.VMEM(down.shape, jnp.float32),
            dma((width // tile,)),
            dma((slots, pieces)),
            dma((3,)),
        ],
        compiler_params=pltpu.CompilerParams(vmem_limit_bytes=60 * 1024 * 1024),
        cost_estimate=pl.CostEstimate(
            flops=2 * depth * count * width, bytes_accessed=4 * count * width, transcendentals=0
        ),
    )(turned, rows, factor, down)


def local(tokens, routes, slot_ids, gate_weight, up_weight):
    width = tokens.shape[1]
    owners = lax.axis_size("expert")
    data_count = lax.axis_size("dp")
    rows, down, factor, turned = gather(
        routes.T, slot_ids.T, tokens, gate_weight[0], up_weight[0], data_count, owners
    )
    count = width // data_count
    if turned.shape[0] != count:
        turned = lax.dynamic_slice_in_dim(rows, lax.axis_index("dp") * count, count, 1).T
    if down.ndim == 3:
        down = jnp.transpose(down, (1, 0, 2)).reshape(down.shape[1], -1)
    input_block, down_block = gram(turned, rows, factor, down)
    return (input_block[None], down_block[None])


def solution(mesh):
    in_specs = (
        P(("dp", "expert"), None),
        P(("dp", "expert"), None),
        P(("dp", "expert"), None),
        P("expert", "dp", None),
        P("expert", "dp", None),
    )
    out_specs = (P("expert", "dp", None), P("expert", "dp", None))
    return jax.shard_map(local, mesh=mesh, in_specs=in_specs, out_specs=out_specs, check_vma=False)
```

```python
import functools

import jax
import jax.numpy as jnp
from jax import lax
from jax.experimental import pallas as pl
from jax.experimental.pallas import tpu as pltpu
from jax.sharding import PartitionSpec as P

CAP = 16
MESH = pl.DeviceIdType.MESH


def peer(e, k, owners):
    return ((e // 2 + k // 2) % (owners // 2)) * 2 + (e + k) % 2


def gather_kernel(n, owners, route_ref, slot_ref, tok_ref, gate_ref, up_ref,
                  x_ref, down_ref, factor_ref, turned_ref,
                  xbuf, sbuf, tok, wg, wu, acc_g, acc_u, hbuf, mine, turned, dpart, counts, held_counts,
                  tok_sem, w_sem, out_sem, down_sem, ex_send, ex_recv, cx_send, cx_recv,
                  ring_send, ring_recv, hid_send, hid_recv, cnt_send, cnt_recv):
    width = tok_ref.shape[1]
    block = owners * CAP
    half = n // 2
    me, e = lax.axis_index("dp"), lax.axis_index("expert")

    odd = me % 2
    pos = (1 - odd) * (me // 2) + odd * (n - 1 - me // 2)

    def at(p):
        late = p // half
        return (1 - late) * (2 * p) + late * (2 * (n - 1 - p) + 1)

    near = (at((pos + 1) % n), at((pos + n - 1) % n))

    step_cols = 1024 if width % 1024 == 0 else 128

    def panel(j):
        cols = pl.ds(pl.multiple_of(j * step_cols, step_cols), step_cols)
        return pltpu.make_async_copy(tok_ref.at[:, cols], tok.at[:, cols], tok_sem.at[j])

    for j in range(width // step_cols):
        panel(j).start()

    barrier = pltpu.get_barrier_semaphore()
    for k in range(1, owners):
        pl.semaphore_signal(barrier, inc=1, device_id=(me, peer(e, k, owners)), device_id_type=MESH)
    for other in near:
        pl.semaphore_signal(barrier, inc=1, device_id=(other, e), device_id_type=MESH)

    loads = [
        pltpu.make_async_copy(gate_ref, wg, w_sem.at[0]),
        pltpu.make_async_copy(up_ref, wu, w_sem.at[1]),
    ]

    slot_rows = lax.broadcasted_iota(jnp.int32, (CAP, tok_ref.shape[0]), 0)
    picks = []
    for k in range(owners):
        wanted = peer(e, k, owners)
        pick = jnp.zeros(slot_rows.shape, jnp.float32)
        for i in range(route_ref.shape[0]):
            hit = (route_ref[i:i + 1, :] == wanted) & (slot_ref[i:i + 1, :] == slot_rows)
            pick = jnp.where(hit, 1.0, pick)
        picks.append(pick)
        counts[k] = jnp.broadcast_to(jnp.sum(pick, axis=(0, 1), keepdims=True), counts.shape[1:])
    hot = jnp.concatenate(picks, axis=0).astype(jnp.bfloat16)

    def dispatch(j, carry):
        cols = pl.ds(pl.multiple_of(j * step_cols, step_cols), step_cols)
        panel(j).wait()
        rows = jnp.dot(hot, tok[:, cols], preferred_element_type=jnp.float32)
        rows = rows.astype(jnp.bfloat16)
        xbuf[0:CAP, cols] = rows[0:CAP]
        sbuf[:, cols] = rows[CAP:]
        return carry

    pending = []
    arrive = {}

    def send(key, src, dst, send_sem, recv_sem, target):
        copy = pltpu.make_async_remote_copy(
            src_ref=src, dst_ref=dst, send_sem=send_sem, recv_sem=recv_sem,
            device_id=target, device_id_type=MESH,
        )
        copy.start()
        pending.append(copy)
        arrive[key] = copy

    panels = width // step_cols
    cut = (panels + 1) // 2
    lax.fori_loop(0, cut, dispatch, 0)
    pl.semaphore_wait(barrier, owners + 1)
    left, right = pl.ds(0, cut * step_cols), pl.ds(cut * step_cols, (panels - cut) * step_cols)
    for d in (0, 1):
        send(("x", d, 1, "first"), xbuf.at[pl.ds(0, CAP), left], xbuf.at[pl.ds((1 + d) * block, CAP), left],
             ring_send.at[d, 0, 0], ring_recv.at[d, 0, 0], (near[d], e))
    lax.fori_loop(cut, panels, dispatch, 0)
    for d in (0, 1):
        send(("x", d, 1, 0), xbuf.at[pl.ds(0, CAP), right], xbuf.at[pl.ds((1 + d) * block, CAP), right],
             ring_send.at[d, 1, 0], ring_recv.at[d, 1, 0], (near[d], e))
    for load in loads:
        load.start()

    stores = []

    for k in range(1, owners):
        other = (me, peer(e, k, owners))
        send(("x", 0, 0, k), sbuf.at[pl.ds((k - 1) * CAP, CAP)], xbuf.at[pl.ds(k * CAP, CAP)],
             ex_send.at[k], ex_recv.at[k], other)
    for k in range(1, owners):
        other = (me, peer(e, k, owners))
        send(("c", 0, k), counts.at[k], held_counts.at[k], cx_send.at[k], cx_recv.at[k], other)

    def slot(d, s):
        if s == 0:
            return 0
        return n - 1 if s == half else 2 * s - 1 + d

    offsets = [0] * n
    for s in range(1, half):
        offsets[slot(0, s)] = n - s
        offsets[slot(1, s)] = s
    offsets[n - 1] = half
    slot_of = [offsets.index(o) for o in range(n)]

    def forward(d, s, c):
        send(("x", d, s, c),
             xbuf.at[pl.ds(slot(d, s - 1) * block + c * CAP, CAP)],
             xbuf.at[pl.ds(slot(d, s) * block + c * CAP, CAP)],
             ring_send.at[d, s, c], ring_recv.at[d, s, c], (near[d], e))

    ends = sorted({max(1, half * (i + 1) // 4) for i in range(4)})
    bounds = [0] + [n if s == half else 2 * s + 1 for s in ends]
    groups = len(bounds) - 1

    def forward_hidden(d, s, g):
        rows = pl.ds(bounds[g] * block, (bounds[g + 1] - bounds[g]) * block)
        send(("h", d, s, g), hbuf.at[slot(d, s - 1), rows], hbuf.at[slot(d, s), rows],
             hid_send.at[d, s, g], hid_recv.at[d, s, g], (near[d], e))

    def ways(s, g):
        return (0, 1) if s < half else (g % 2,)

    def forward_counts(d, s):
        send(("n", d, s), counts.at[owners + slot(d, s - 1)], counts.at[owners + slot(d, s)],
             cnt_send.at[d, s], cnt_recv.at[d, s], (near[d], e))

    def hidden(first, count):
        rows = count * block
        base = first * block
        acc_g[0:rows, :] = jnp.zeros((rows, acc_g.shape[1]), jnp.float32)
        acc_u[0:rows, :] = jnp.zeros((rows, acc_u.shape[1]), jnp.float32)

        def body(j, carry):
            cols = pl.ds(pl.multiple_of(j * step_cols, step_cols), step_cols)
            part = xbuf[base:base + rows, cols]
            dims = (((1,), (1,)), ((), ()))
            acc_g[0:rows, :] += lax.dot_general(part, wg[:, cols], dims, preferred_element_type=jnp.float32)
            acc_u[0:rows, :] += lax.dot_general(part, wu[:, cols], dims, preferred_element_type=jnp.float32)
            return carry

        lax.fori_loop(0, width // step_cols, body, 0)
        gate = acc_g[0:rows, :]
        out = (gate / (1.0 + jnp.exp(-gate)) * acc_u[0:rows, :]).astype(jnp.bfloat16)
        hbuf[0, base:base + rows, :] = out

    def down(d, s):
        j = slot(d, s)
        for r in range(n):
            own = slot_of[(offsets[j] + offsets[r]) % n]
            mine[r * block:(r + 1) * block, :] = hbuf[0, own * block:(own + 1) * block, :]
        part = factor_ref[0:1, 0:1] * lax.dot_general(
            mine[...], hbuf[j], (((0,), (0,)), ((), ())), preferred_element_type=jnp.float32
        )
        place = at((pos + offsets[j]) % n)
        dpart[j] = part
        if len(down_ref.shape) == 2:
            units = down_ref.shape[0]
            target = down_ref.at[:, pl.ds(pl.multiple_of(place * units, units), units)]
        else:
            target = down_ref.at[place]
        copy = pltpu.make_async_copy(dpart.at[j], target, down_sem.at[j])
        copy.start()
        stores.append(copy)

    def keep(first, count):
        rows = pl.ds(first * block, count * block)
        copy = pltpu.make_async_copy(xbuf.at[rows], x_ref.at[rows], out_sem.at[first])
        copy.start()
        stores.append(copy)

    for s in range(1, half + 1):
        for c in range(owners):
            if s == 1:
                if c > 0:
                    arrive[("x", 0, 0, c)].wait_recv()
            else:
                if s == 2 and c == 0:
                    arrive[("x", 0, 1, "first")].wait_recv()
                    arrive[("x", 1, 1, "first")].wait_recv()
                arrive[("x", 0, s - 1, c)].wait_recv()
                arrive[("x", 1, s - 1, c)].wait_recv()
            if s == 1 and c == 0:
                pass
            elif s < half:
                forward(0, s, c)
                forward(1, s, c)
            else:
                forward(0 if c < owners // 2 else 1, s, c)
        if s == 1:
            total = counts[0]
            for k in range(1, owners):
                arrive[("c", 0, k)].wait_recv()
                total = total + held_counts[k]
            counts[owners] = total
            forward_counts(0, 1)
            forward_counts(1, 1)
            keep(0, 1)
            for load in loads:
                load.wait()
            hidden(0, 1)
        else:
            arrive[("n", 0, s - 1)].wait_recv()
            arrive[("n", 1, s - 1)].wait_recv()
            forward_counts(0, s)
            if s < half:
                forward_counts(1, s)
            if s == half:
                for g in range(groups - 2):
                    forward_hidden(0, 1, g)
                    forward_hidden(1, 1, g)
            first = slot(0, s - 1)
            keep(first, 2)
            hidden(first, 2)
    if groups > 1:
        forward_hidden(0, 1, groups - 2)
        forward_hidden(1, 1, groups - 2)
    for c in range(owners):
        arrive[("x", 0 if c < owners // 2 else 1, half, c)].wait_recv()
    keep(n - 1, 1)

    def pass_on(s, g):
        for d in ways(s, g):
            arrive[("h", d, s, g)].wait_recv()
        if s < half:
            for d in ways(s + 1, g):
                forward_hidden(d, s + 1, g)

    for g in range(groups - 2):
        pass_on(1, g)
    hidden(n - 1, 1)
    forward_hidden(0, 1, groups - 1)
    forward_hidden(1, 1, groups - 1)
    arrive[("n", 0, half)].wait_recv()
    total = counts[owners]
    for j in range(1, n):
        total = total + counts[owners + j]
    factor_ref[...] = 2.0 / total
    down(0, 0)
    for s in range(1, half + 1):
        for g in range(groups):
            if s > 1 or g >= groups - 2:
                pass_on(s, g)
        if s == 2:
            count = turned_ref.shape[0]
            if count == width // n:
                turned[...] = xbuf[:, pl.ds(pl.multiple_of(me * count, 128), count)].T
                copy = pltpu.make_async_copy(turned, turned_ref, down_sem.at[n])
                copy.start()
                stores.append(copy)
        down(0, s)
        if s < half:
            down(1, s)
    for copy in pending:
        copy.wait_send()
    for copy in stores:
        copy.wait()


def gather(routes_t, slots_t, tokens, gate_rows, up_rows, n, owners):
    width = tokens.shape[1]
    units = gate_rows.shape[0]
    block = owners * CAP
    half = n // 2
    vmem = pl.BlockSpec(memory_space=pltpu.VMEM)
    hbm = pl.BlockSpec(memory_space=pl.ANY)
    rows = n * block
    dma = pltpu.SemaphoreType.DMA
    return pl.pallas_call(
        functools.partial(gather_kernel, n, owners),
        out_shape=(
            jax.ShapeDtypeStruct((rows, width), jnp.bfloat16),
            jax.ShapeDtypeStruct((units, n * units) if units % 128 == 0 else (n, units, units), jnp.float32),
            jax.ShapeDtypeStruct((8, 128), jnp.float32),
            jax.ShapeDtypeStruct((width // n, rows) if (width // n) % 128 == 0 else (8, 128), jnp.bfloat16),
        ),
        in_specs=[vmem, vmem, hbm, hbm, hbm],
        out_specs=(hbm, hbm, vmem, hbm),
        scratch_shapes=[
            pltpu.VMEM((rows, width), jnp.bfloat16),
            pltpu.VMEM((block - CAP, width), jnp.bfloat16),
            pltpu.VMEM(tokens.shape, jnp.bfloat16),
            pltpu.VMEM((units, width), jnp.bfloat16),
            pltpu.VMEM((units, width), jnp.bfloat16),
            pltpu.VMEM((2 * block, units), jnp.float32),
            pltpu.VMEM((2 * block, units), jnp.float32),
            pltpu.VMEM((n, rows, units), jnp.bfloat16),
            pltpu.VMEM((rows, units), jnp.bfloat16),
            pltpu.VMEM((width // n, rows) if (width // n) % 128 == 0 else (8, 128), jnp.bfloat16),
            pltpu.VMEM((n, units, units), jnp.float32),
            pltpu.VMEM((owners + n, 8, 128), jnp.float32),
            pltpu.VMEM((owners, 8, 128), jnp.float32),
            dma((width // (1024 if width % 1024 == 0 else 128),)),
            dma((2,)),
            dma((n,)),
            dma((n + 1,)),
            dma((owners,)),
            dma((owners,)),
            dma((owners,)),
            dma((owners,)),
            dma((2, half + 1, owners)),
            dma((2, half + 1, owners)),
            dma((2, half + 1, 4)),
            dma((2, half + 1, 4)),
            dma((2, half + 1)),
            dma((2, half + 1)),
        ],
        compiler_params=pltpu.CompilerParams(
            collective_id=0, has_side_effects=True, vmem_limit_bytes=60 * 1024 * 1024
        ),
        cost_estimate=pl.CostEstimate(
            flops=4 * rows * width * units, bytes_accessed=6 * rows * width, transcendentals=rows * units
        ),
    )(routes_t, slots_t, tokens, gate_rows, up_rows)


def gram_kernel(tile, pieces, turned_ref, rows_ref, factor_ref, down_in, out_ref, down_out,
                held, parts, turned, down_held, in_sem, out_sem, own_sem):
    width = rows_ref.shape[1]
    slots, count = parts.shape[0], parts.shape[1]
    steps = width // tile
    piece = count // pieces

    def load(j):
        cols = pl.ds(pl.multiple_of(j * tile, tile), tile)
        return pltpu.make_async_copy(rows_ref.at[:, cols], held.at[:, cols], in_sem.at[j])

    def store(j, i):
        b = j % slots
        rows = pl.ds(i * piece, piece)
        cols = pl.ds(pl.multiple_of(j * tile, tile), tile)
        return pltpu.make_async_copy(parts.at[b, rows], out_ref.at[rows, cols], out_sem.at[b, i])

    turned_load = pltpu.make_async_copy(turned_ref, turned, own_sem.at[0])
    down_load = pltpu.make_async_copy(down_in, down_held, own_sem.at[1])
    down_store = pltpu.make_async_copy(down_held, down_out, own_sem.at[2])
    turned_load.start()
    ahead = min(3, steps)
    for j in range(ahead):
        load(j).start()
    turned_load.wait()

    def body(j, carry):
        load(j).wait()

        @pl.when(j + ahead < steps)
        def _():
            load(j + ahead).start()

        @pl.when(j >= slots)
        def _():
            for i in range(pieces):
                store(j - slots, i).wait()

        cols = pl.ds(pl.multiple_of(j * tile, tile), tile)
        for i in range(pieces):
            rows = slice(i * piece, (i + 1) * piece)
            parts[j % slots, rows] = factor_ref[0:1, 0:1] * jnp.dot(
                turned[rows, :], held[:, cols], preferred_element_type=jnp.float32
            )
            store(j, i).start()
        return carry

    early, late = min(slots, steps), max(min(slots, steps), steps - 3)
    lax.fori_loop(0, early, body, 0)
    down_load.start()
    lax.fori_loop(early, late, body, 0)
    down_load.wait()
    down_store.start()
    lax.fori_loop(late, steps, body, 0)
    for j in range(max(0, steps - slots), steps):
        for i in range(pieces):
            store(j, i).wait()
    down_store.wait()


def gram(turned, rows, factor, down):
    depth, width = rows.shape
    count = turned.shape[0]
    tile = 512 if width % 512 == 0 else 128
    pieces = 2 if count % 16 == 0 else 1
    slots = 4
    vmem = pl.BlockSpec(memory_space=pltpu.VMEM)
    hbm = pl.BlockSpec(memory_space=pl.ANY)
    dma = pltpu.SemaphoreType.DMA
    return pl.pallas_call(
        functools.partial(gram_kernel, tile, pieces),
        out_shape=(
            jax.ShapeDtypeStruct((count, width), jnp.float32),
            jax.ShapeDtypeStruct(down.shape, jnp.float32),
        ),
        in_specs=[hbm, hbm, vmem, hbm],
        out_specs=(hbm, hbm),
        scratch_shapes=[
            pltpu.VMEM((depth, width), jnp.bfloat16),
            pltpu.VMEM((slots, count, tile), jnp.float32),
            pltpu.VMEM(turned.shape, jnp.bfloat16),
            pltpu.VMEM(down.shape, jnp.float32),
            dma((width // tile,)),
            dma((slots, pieces)),
            dma((3,)),
        ],
        compiler_params=pltpu.CompilerParams(vmem_limit_bytes=60 * 1024 * 1024),
        cost_estimate=pl.CostEstimate(
            flops=2 * depth * count * width, bytes_accessed=4 * count * width, transcendentals=0
        ),
    )(turned, rows, factor, down)


def local(tokens, routes, slot_ids, gate_weight, up_weight):
    width = tokens.shape[1]
    owners = lax.axis_size("expert")
    data_count = lax.axis_size("dp")
    rows, down, factor, turned = gather(
        routes.T, slot_ids.T, tokens, gate_weight[0], up_weight[0], data_count, owners
    )
    count = width // data_count
    if turned.shape[0] != count:
        turned = lax.dynamic_slice_in_dim(rows, lax.axis_index("dp") * count, count, 1).T
    if down.ndim == 3:
        down = jnp.transpose(down, (1, 0, 2)).reshape(down.shape[1], -1)
    input_block, down_block = gram(turned, rows, factor, down)
    return (input_block[None], down_block[None])


def solution(mesh):
    in_specs = (
        P(("dp", "expert"), None),
        P(("dp", "expert"), None),
        P(("dp", "expert"), None),
        P("expert", "dp", None),
        P("expert", "dp", None),
    )
    out_specs = (P("expert", "dp", None), P("expert", "dp", None))
    return jax.shard_map(local, mesh=mesh, in_specs=in_specs, out_specs=out_specs, check_vma=False)
```

```python
import functools

import jax
import jax.numpy as jnp
from jax import lax
from jax.experimental import pallas as pl
from jax.experimental.pallas import tpu as pltpu
from jax.sharding import PartitionSpec as P

CAP = 16
MESH = pl.DeviceIdType.MESH


def peer(e, k, owners):
    return ((e // 2 + k // 2) % (owners // 2)) * 2 + (e + k) % 2


def gather_kernel(n, owners, route_ref, slot_ref, tok_ref, gate_ref, up_ref,
                  x_ref, down_ref, factor_ref, turned_ref,
                  xbuf, sbuf, tok, wg, wu, acc_g, acc_u, hbuf, mine, turned, dpart, counts, held_counts,
                  tok_sem, w_sem, out_sem, down_sem, ex_send, ex_recv, cx_send, cx_recv,
                  ring_send, ring_recv, hid_send, hid_recv, cnt_send, cnt_recv):
    width = tok_ref.shape[1]
    block = owners * CAP
    half = n // 2
    me, e = lax.axis_index("dp"), lax.axis_index("expert")

    odd = me % 2
    pos = (1 - odd) * (me // 2) + odd * (n - 1 - me // 2)

    def at(p):
        late = p // half
        return (1 - late) * (2 * p) + late * (2 * (n - 1 - p) + 1)

    near = (at((pos + 1) % n), at((pos + n - 1) % n))

    step_cols = 1024 if width % 1024 == 0 else 128

    def panel(j):
        cols = pl.ds(pl.multiple_of(j * step_cols, step_cols), step_cols)
        return pltpu.make_async_copy(tok_ref.at[:, cols], tok.at[:, cols], tok_sem.at[j])

    for j in range(width // step_cols):
        panel(j).start()

    barrier = pltpu.get_barrier_semaphore()
    for k in range(1, owners):
        pl.semaphore_signal(barrier, inc=1, device_id=(me, peer(e, k, owners)), device_id_type=MESH)
    for other in near:
        pl.semaphore_signal(barrier, inc=1, device_id=(other, e), device_id_type=MESH)

    loads = [
        pltpu.make_async_copy(gate_ref, wg, w_sem.at[0]),
        pltpu.make_async_copy(up_ref, wu, w_sem.at[1]),
    ]

    slot_rows = lax.broadcasted_iota(jnp.int32, (CAP, tok_ref.shape[0]), 0)
    picks = []
    for k in range(owners):
        wanted = peer(e, k, owners)
        pick = jnp.zeros(slot_rows.shape, jnp.float32)
        for i in range(route_ref.shape[0]):
            hit = (route_ref[i:i + 1, :] == wanted) & (slot_ref[i:i + 1, :] == slot_rows)
            pick = jnp.where(hit, 1.0, pick)
        picks.append(pick)
        counts[k] = jnp.broadcast_to(jnp.sum(pick, axis=(0, 1), keepdims=True), counts.shape[1:])
    hot = jnp.concatenate(picks, axis=0).astype(jnp.bfloat16)

    def dispatch(j, carry):
        cols = pl.ds(pl.multiple_of(j * step_cols, step_cols), step_cols)
        panel(j).wait()
        rows = jnp.dot(hot, tok[:, cols], preferred_element_type=jnp.float32)
        rows = rows.astype(jnp.bfloat16)
        xbuf[0:CAP, cols] = rows[0:CAP]
        sbuf[:, cols] = rows[CAP:]
        return carry

    pending = []
    arrive = {}

    def send(key, src, dst, send_sem, recv_sem, target):
        copy = pltpu.make_async_remote_copy(
            src_ref=src, dst_ref=dst, send_sem=send_sem, recv_sem=recv_sem,
            device_id=target, device_id_type=MESH,
        )
        copy.start()
        pending.append(copy)
        arrive[key] = copy

    panels = width // step_cols
    cut = (panels + 1) // 2
    lax.fori_loop(0, cut, dispatch, 0)
    pl.semaphore_wait(barrier, owners + 1)
    left, right = pl.ds(0, cut * step_cols), pl.ds(cut * step_cols, (panels - cut) * step_cols)
    for d in (0, 1):
        send(("x", d, 1, "first"), xbuf.at[pl.ds(0, CAP), left], xbuf.at[pl.ds((1 + d) * block, CAP), left],
             ring_send.at[d, 0, 0], ring_recv.at[d, 0, 0], (near[d], e))
    lax.fori_loop(cut, panels, dispatch, 0)
    for d in (0, 1):
        send(("x", d, 1, 0), xbuf.at[pl.ds(0, CAP), right], xbuf.at[pl.ds((1 + d) * block, CAP), right],
             ring_send.at[d, 1, 0], ring_recv.at[d, 1, 0], (near[d], e))
    for load in loads:
        load.start()

    stores = []

    def exchange(k):
        other = (me, peer(e, k, owners))
        send(("x", 0, 0, k), sbuf.at[pl.ds((k - 1) * CAP, CAP)], xbuf.at[pl.ds(k * CAP, CAP)],
             ex_send.at[k], ex_recv.at[k], other)

    for k in range(1, owners - 1):
        exchange(k)
    for k in range(1, owners):
        other = (me, peer(e, k, owners))
        send(("c", 0, k), counts.at[k], held_counts.at[k], cx_send.at[k], cx_recv.at[k], other)

    def slot(d, s):
        if s == 0:
            return 0
        return n - 1 if s == half else 2 * s - 1 + d

    offsets = [0] * n
    for s in range(1, half):
        offsets[slot(0, s)] = n - s
        offsets[slot(1, s)] = s
    offsets[n - 1] = half
    slot_of = [offsets.index(o) for o in range(n)]

    def forward(d, s, c):
        send(("x", d, s, c),
             xbuf.at[pl.ds(slot(d, s - 1) * block + c * CAP, CAP)],
             xbuf.at[pl.ds(slot(d, s) * block + c * CAP, CAP)],
             ring_send.at[d, s, c], ring_recv.at[d, s, c], (near[d], e))

    ends = sorted({max(1, half * (i + 1) // 4) for i in range(4)})
    bounds = [0] + [n if s == half else 2 * s + 1 for s in ends]
    groups = len(bounds) - 1

    def forward_hidden(d, s, g):
        rows = pl.ds(bounds[g] * block, (bounds[g + 1] - bounds[g]) * block)
        send(("h", d, s, g), hbuf.at[slot(d, s - 1), rows], hbuf.at[slot(d, s), rows],
             hid_send.at[d, s, g], hid_recv.at[d, s, g], (near[d], e))

    def ways(s, g):
        return (0, 1) if s < half else ((0,) if g in (0, 3) else (1,))

    def forward_counts(d, s):
        send(("n", d, s), counts.at[owners + slot(d, s - 1)], counts.at[owners + slot(d, s)],
             cnt_send.at[d, s], cnt_recv.at[d, s], (near[d], e))

    def hidden(first, count):
        rows = count * block
        base = first * block
        acc_g[0:rows, :] = jnp.zeros((rows, acc_g.shape[1]), jnp.float32)
        acc_u[0:rows, :] = jnp.zeros((rows, acc_u.shape[1]), jnp.float32)

        def body(j, carry):
            cols = pl.ds(pl.multiple_of(j * step_cols, step_cols), step_cols)
            part = xbuf[base:base + rows, cols]
            dims = (((1,), (1,)), ((), ()))
            acc_g[0:rows, :] += lax.dot_general(part, wg[:, cols], dims, preferred_element_type=jnp.float32)
            acc_u[0:rows, :] += lax.dot_general(part, wu[:, cols], dims, preferred_element_type=jnp.float32)
            return carry

        lax.fori_loop(0, width // step_cols, body, 0)
        gate = acc_g[0:rows, :]
        out = (gate / (1.0 + jnp.exp(-gate)) * acc_u[0:rows, :]).astype(jnp.bfloat16)
        hbuf[0, base:base + rows, :] = out

    def arrange(j):
        for r in range(n):
            own = slot_of[(offsets[j] + offsets[r]) % n]
            mine[r * block:(r + 1) * block, :] = hbuf[0, own * block:(own + 1) * block, :]

    def down(d, s):
        j = slot(d, s)
        if s < half:
            arrange(j)
        part = factor_ref[0:1, 0:1] * lax.dot_general(
            mine[...], hbuf[j], (((0,), (0,)), ((), ())), preferred_element_type=jnp.float32
        )
        place = at((pos + offsets[j]) % n)
        dpart[j] = part
        if len(down_ref.shape) == 2:
            units = down_ref.shape[0]
            target = down_ref.at[:, pl.ds(pl.multiple_of(place * units, units), units)]
        else:
            target = down_ref.at[place]
        copy = pltpu.make_async_copy(dpart.at[j], target, down_sem.at[j])
        copy.start()
        stores.append(copy)

    def keep(first, count):
        rows = pl.ds(first * block, count * block)
        copy = pltpu.make_async_copy(xbuf.at[rows], x_ref.at[rows], out_sem.at[first])
        copy.start()
        stores.append(copy)

    for s in range(1, half + 1):
        for c in range(owners):
            if s == 1:
                if c == owners - 2:
                    held_back = arrive[("x", 0, 0, c)]
                    held_back.wait_send()
                    pending[:] = [copy for copy in pending if copy is not held_back]
                    exchange(owners - 1)
                if c > 0:
                    arrive[("x", 0, 0, c)].wait_recv()
            else:
                if s == 2 and c == 0:
                    arrive[("x", 0, 1, "first")].wait_recv()
                    arrive[("x", 1, 1, "first")].wait_recv()
                arrive[("x", 0, s - 1, c)].wait_recv()
                arrive[("x", 1, s - 1, c)].wait_recv()
            if s == 1 and c == 0:
                pass
            elif s < half:
                forward(0, s, c)
                forward(1, s, c)
            else:
                forward(0 if c < owners // 2 else 1, s, c)
        if s == 1:
            total = counts[0]
            for k in range(1, owners):
                arrive[("c", 0, k)].wait_recv()
                total = total + held_counts[k]
            counts[owners] = total
            forward_counts(0, 1)
            forward_counts(1, 1)
            keep(0, 1)
            for load in loads:
                load.wait()
            hidden(0, 1)
        else:
            arrive[("n", 0, s - 1)].wait_recv()
            arrive[("n", 1, s - 1)].wait_recv()
            forward_counts(0, s)
            if s < half:
                forward_counts(1, s)
            if s == half:
                for g in range(groups - 2):
                    forward_hidden(0, 1, g)
                    forward_hidden(1, 1, g)
            first = slot(0, s - 1)
            keep(first, 2)
            hidden(first, 2)
    if groups > 1:
        forward_hidden(0, 1, groups - 2)
        forward_hidden(1, 1, groups - 2)
    for c in range(owners):
        arrive[("x", 0 if c < owners // 2 else 1, half, c)].wait_recv()
    keep(n - 1, 1)

    def pass_on(s, g):
        for d in ways(s, g):
            arrive[("h", d, s, g)].wait_recv()
        if s < half:
            for d in ways(s + 1, g):
                forward_hidden(d, s + 1, g)

    for g in range(groups - 2):
        pass_on(1, g)
    hidden(n - 1, 1)
    forward_hidden(0, 1, groups - 1)
    forward_hidden(1, 1, groups - 1)
    arrive[("n", 0, half)].wait_recv()
    total = counts[owners]
    for j in range(1, n):
        total = total + counts[owners + j]
    factor_ref[...] = 2.0 / total
    down(0, 0)
    for s in range(1, half + 1):
        if s == half:
            arrange(n - 1)
        for g in range(groups):
            if s > 1 or g >= groups - 2:
                pass_on(s, g)
        if s == 2:
            count = turned_ref.shape[0]
            if count == width // n:
                turned[...] = xbuf[:, pl.ds(pl.multiple_of(me * count, 128), count)].T
                copy = pltpu.make_async_copy(turned, turned_ref, down_sem.at[n])
                copy.start()
                stores.append(copy)
        down(0, s)
        if s < half:
            down(1, s)
    for copy in pending:
        copy.wait_send()
    for copy in stores:
        copy.wait()


def gather(routes_t, slots_t, tokens, gate_rows, up_rows, n, owners):
    width = tokens.shape[1]
    units = gate_rows.shape[0]
    block = owners * CAP
    half = n // 2
    vmem = pl.BlockSpec(memory_space=pltpu.VMEM)
    hbm = pl.BlockSpec(memory_space=pl.ANY)
    rows = n * block
    dma = pltpu.SemaphoreType.DMA
    return pl.pallas_call(
        functools.partial(gather_kernel, n, owners),
        out_shape=(
            jax.ShapeDtypeStruct((rows, width), jnp.bfloat16),
            jax.ShapeDtypeStruct((units, n * units) if units % 128 == 0 else (n, units, units), jnp.float32),
            jax.ShapeDtypeStruct((8, 128), jnp.float32),
            jax.ShapeDtypeStruct((width // n, rows) if (width // n) % 128 == 0 else (8, 128), jnp.bfloat16),
        ),
        in_specs=[vmem, vmem, hbm, hbm, hbm],
        out_specs=(hbm, hbm, vmem, hbm),
        scratch_shapes=[
            pltpu.VMEM((rows, width), jnp.bfloat16),
            pltpu.VMEM((block - CAP, width), jnp.bfloat16),
            pltpu.VMEM(tokens.shape, jnp.bfloat16),
            pltpu.VMEM((units, width), jnp.bfloat16),
            pltpu.VMEM((units, width), jnp.bfloat16),
            pltpu.VMEM((2 * block, units), jnp.float32),
            pltpu.VMEM((2 * block, units), jnp.float32),
            pltpu.VMEM((n, rows, units), jnp.bfloat16),
            pltpu.VMEM((rows, units), jnp.bfloat16),
            pltpu.VMEM((width // n, rows) if (width // n) % 128 == 0 else (8, 128), jnp.bfloat16),
            pltpu.VMEM((n, units, units), jnp.float32),
            pltpu.VMEM((owners + n, 8, 128), jnp.float32),
            pltpu.VMEM((owners, 8, 128), jnp.float32),
            dma((width // (1024 if width % 1024 == 0 else 128),)),
            dma((2,)),
            dma((n,)),
            dma((n + 1,)),
            dma((owners,)),
            dma((owners,)),
            dma((owners,)),
            dma((owners,)),
            dma((2, half + 1, owners)),
            dma((2, half + 1, owners)),
            dma((2, half + 1, 4)),
            dma((2, half + 1, 4)),
            dma((2, half + 1)),
            dma((2, half + 1)),
        ],
        compiler_params=pltpu.CompilerParams(
            collective_id=0, has_side_effects=True, vmem_limit_bytes=60 * 1024 * 1024
        ),
        cost_estimate=pl.CostEstimate(
            flops=4 * rows * width * units, bytes_accessed=6 * rows * width, transcendentals=rows * units
        ),
    )(routes_t, slots_t, tokens, gate_rows, up_rows)


def gram_kernel(tile, pieces, turned_ref, rows_ref, factor_ref, down_in, out_ref, down_out,
                held, parts, turned, down_held, in_sem, out_sem, own_sem):
    width = rows_ref.shape[1]
    slots, count = parts.shape[0], parts.shape[1]
    steps = width // tile
    piece = count // pieces

    def load(j):
        cols = pl.ds(pl.multiple_of(j * tile, tile), tile)
        return pltpu.make_async_copy(rows_ref.at[:, cols], held.at[:, cols], in_sem.at[j])

    def store(j, i):
        b = j % slots
        rows = pl.ds(i * piece, piece)
        cols = pl.ds(pl.multiple_of(j * tile, tile), tile)
        return pltpu.make_async_copy(parts.at[b, rows], out_ref.at[rows, cols], out_sem.at[b, i])

    turned_load = pltpu.make_async_copy(turned_ref, turned, own_sem.at[0])
    down_load = pltpu.make_async_copy(down_in, down_held, own_sem.at[1])
    down_store = pltpu.make_async_copy(down_held, down_out, own_sem.at[2])
    turned_load.start()
    ahead = min(3, steps)
    for j in range(ahead):
        load(j).start()
    turned_load.wait()

    def body(j, carry):
        load(j).wait()

        @pl.when(j + ahead < steps)
        def _():
            load(j + ahead).start()

        @pl.when(j >= slots)
        def _():
            for i in range(pieces):
                store(j - slots, i).wait()

        cols = pl.ds(pl.multiple_of(j * tile, tile), tile)
        for i in range(pieces):
            rows = slice(i * piece, (i + 1) * piece)
            parts[j % slots, rows] = factor_ref[0:1, 0:1] * jnp.dot(
                turned[rows, :], held[:, cols], preferred_element_type=jnp.float32
            )
            store(j, i).start()
        return carry

    early, late = min(slots, steps), max(min(slots, steps), steps - 3)
    lax.fori_loop(0, early, body, 0)
    down_load.start()
    lax.fori_loop(early, late, body, 0)
    down_load.wait()
    down_store.start()
    lax.fori_loop(late, steps, body, 0)
    for j in range(max(0, steps - slots), steps):
        for i in range(pieces):
            store(j, i).wait()
    down_store.wait()


def gram(turned, rows, factor, down):
    depth, width = rows.shape
    count = turned.shape[0]
    tile = 512 if width % 512 == 0 else 128
    pieces = 2 if count % 16 == 0 else 1
    slots = 4
    vmem = pl.BlockSpec(memory_space=pltpu.VMEM)
    hbm = pl.BlockSpec(memory_space=pl.ANY)
    dma = pltpu.SemaphoreType.DMA
    return pl.pallas_call(
        functools.partial(gram_kernel, tile, pieces),
        out_shape=(
            jax.ShapeDtypeStruct((count, width), jnp.float32),
            jax.ShapeDtypeStruct(down.shape, jnp.float32),
        ),
        in_specs=[hbm, hbm, vmem, hbm],
        out_specs=(hbm, hbm),
        scratch_shapes=[
            pltpu.VMEM((depth, width), jnp.bfloat16),
            pltpu.VMEM((slots, count, tile), jnp.float32),
            pltpu.VMEM(turned.shape, jnp.bfloat16),
            pltpu.VMEM(down.shape, jnp.float32),
            dma((width // tile,)),
            dma((slots, pieces)),
            dma((3,)),
        ],
        compiler_params=pltpu.CompilerParams(vmem_limit_bytes=60 * 1024 * 1024),
        cost_estimate=pl.CostEstimate(
            flops=2 * depth * count * width, bytes_accessed=4 * count * width, transcendentals=0
        ),
    )(turned, rows, factor, down)


def local(tokens, routes, slot_ids, gate_weight, up_weight):
    width = tokens.shape[1]
    owners = lax.axis_size("expert")
    data_count = lax.axis_size("dp")
    rows, down, factor, turned = gather(
        routes.T, slot_ids.T, tokens, gate_weight[0], up_weight[0], data_count, owners
    )
    count = width // data_count
    if turned.shape[0] != count:
        turned = lax.dynamic_slice_in_dim(rows, lax.axis_index("dp") * count, count, 1).T
    if down.ndim == 3:
        down = jnp.transpose(down, (1, 0, 2)).reshape(down.shape[1], -1)
    input_block, down_block = gram(turned, rows, factor, down)
    return (input_block[None], down_block[None])


def solution(mesh):
    in_specs = (
        P(("dp", "expert"), None),
        P(("dp", "expert"), None),
        P(("dp", "expert"), None),
        P("expert", "dp", None),
        P("expert", "dp", None),
    )
    out_specs = (P("expert", "dp", None), P("expert", "dp", None))
    return jax.shard_map(local, mesh=mesh, in_specs=in_specs, out_specs=out_specs, check_vma=False)
```

```python
import functools

import jax
import jax.numpy as jnp
from jax import lax
from jax.experimental import pallas as pl
from jax.experimental.pallas import tpu as pltpu
from jax.sharding import PartitionSpec as P

CAP = 16
MESH = pl.DeviceIdType.MESH


def peer(e, k, owners):
    return ((e // 2 + k // 2) % (owners // 2)) * 2 + (e + k) % 2


def gather_kernel(n, owners, route_ref, slot_ref, tok_ref, gate_ref, up_ref,
                  x_ref, down_ref, factor_ref, turned_ref,
                  xbuf, sbuf, tok, wg, wu, acc_g, acc_u, hbuf, mine, turned, dpart, counts, held_counts,
                  tok_sem, w_sem, out_sem, down_sem, ex_send, ex_recv, cx_send, cx_recv,
                  ring_send, ring_recv, hid_send, hid_recv, cnt_send, cnt_recv):
    width = tok_ref.shape[1]
    block = owners * CAP
    half = n // 2
    me, e = lax.axis_index("dp"), lax.axis_index("expert")

    odd = me % 2
    pos = (1 - odd) * (me // 2) + odd * (n - 1 - me // 2)

    def at(p):
        late = p // half
        return (1 - late) * (2 * p) + late * (2 * (n - 1 - p) + 1)

    near = (at((pos + 1) % n), at((pos + n - 1) % n))

    step_cols = 1024 if width % 1024 == 0 else 128

    def panel(j):
        cols = pl.ds(pl.multiple_of(j * step_cols, step_cols), step_cols)
        return pltpu.make_async_copy(tok_ref.at[:, cols], tok.at[:, cols], tok_sem.at[j])

    for j in range(width // step_cols):
        panel(j).start()

    barrier = pltpu.get_barrier_semaphore()
    for k in range(1, owners):
        pl.semaphore_signal(barrier, inc=1, device_id=(me, peer(e, k, owners)), device_id_type=MESH)
    for other in near:
        pl.semaphore_signal(barrier, inc=1, device_id=(other, e), device_id_type=MESH)

    loads = [
        pltpu.make_async_copy(gate_ref, wg, w_sem.at[0]),
        pltpu.make_async_copy(up_ref, wu, w_sem.at[1]),
    ]

    slot_rows = lax.broadcasted_iota(jnp.int32, (CAP, tok_ref.shape[0]), 0)
    picks = []
    for k in range(owners):
        wanted = peer(e, k, owners)
        pick = jnp.zeros(slot_rows.shape, jnp.float32)
        for i in range(route_ref.shape[0]):
            hit = (route_ref[i:i + 1, :] == wanted) & (slot_ref[i:i + 1, :] == slot_rows)
            pick = jnp.where(hit, 1.0, pick)
        picks.append(pick)
        counts[k] = jnp.broadcast_to(jnp.sum(pick, axis=(0, 1), keepdims=True), counts.shape[1:])
    hot = jnp.concatenate(picks, axis=0).astype(jnp.bfloat16)

    def dispatch(j, carry):
        cols = pl.ds(pl.multiple_of(j * step_cols, step_cols), step_cols)
        panel(j).wait()
        rows = jnp.dot(hot, tok[:, cols], preferred_element_type=jnp.float32)
        rows = rows.astype(jnp.bfloat16)
        xbuf[0:CAP, cols] = rows[0:CAP]
        sbuf[:, cols] = rows[CAP:]
        return carry

    pending = []
    arrive = {}

    def send(key, src, dst, send_sem, recv_sem, target):
        copy = pltpu.make_async_remote_copy(
            src_ref=src, dst_ref=dst, send_sem=send_sem, recv_sem=recv_sem,
            device_id=target, device_id_type=MESH,
        )
        copy.start()
        pending.append(copy)
        arrive[key] = copy

    panels = width // step_cols
    cut = (panels + 1) // 2
    lax.fori_loop(0, cut, dispatch, 0)
    pl.semaphore_wait(barrier, owners + 1)
    left, right = pl.ds(0, cut * step_cols), pl.ds(cut * step_cols, (panels - cut) * step_cols)
    for d in (0, 1):
        send(("x", d, 1, "first"), xbuf.at[pl.ds(0, CAP), left], xbuf.at[pl.ds((1 + d) * block, CAP), left],
             ring_send.at[d, 0, 0], ring_recv.at[d, 0, 0], (near[d], e))
    lax.fori_loop(cut, panels, dispatch, 0)
    for d in (0, 1):
        send(("x", d, 1, 0), xbuf.at[pl.ds(0, CAP), right], xbuf.at[pl.ds((1 + d) * block, CAP), right],
             ring_send.at[d, 1, 0], ring_recv.at[d, 1, 0], (near[d], e))
    for load in loads:
        load.start()

    stores = []

    def exchange(k):
        other = (me, peer(e, k, owners))
        send(("x", 0, 0, k), sbuf.at[pl.ds((k - 1) * CAP, CAP)], xbuf.at[pl.ds(k * CAP, CAP)],
             ex_send.at[k], ex_recv.at[k], other)

    for k in range(1, owners - 1):
        exchange(k)
    for k in range(1, owners):
        other = (me, peer(e, k, owners))
        send(("c", 0, k), counts.at[k], held_counts.at[k], cx_send.at[k], cx_recv.at[k], other)

    def slot(d, s):
        if s == 0:
            return 0
        return n - 1 if s == half else 2 * s - 1 + d

    offsets = [0] * n
    for s in range(1, half):
        offsets[slot(0, s)] = n - s
        offsets[slot(1, s)] = s
    offsets[n - 1] = half
    slot_of = [offsets.index(o) for o in range(n)]

    def forward(d, s, c):
        send(("x", d, s, c),
             xbuf.at[pl.ds(slot(d, s - 1) * block + c * CAP, CAP)],
             xbuf.at[pl.ds(slot(d, s) * block + c * CAP, CAP)],
             ring_send.at[d, s, c], ring_recv.at[d, s, c], (near[d], e))

    ends = sorted({max(1, half * (i + 1) // 4) for i in range(4)})
    bounds = [0] + [n if s == half else 2 * s + 1 for s in ends]
    groups = len(bounds) - 1

    def forward_hidden(d, s, g):
        rows = pl.ds(bounds[g] * block, (bounds[g + 1] - bounds[g]) * block)
        send(("h", d, s, g), hbuf.at[slot(d, s - 1), rows], hbuf.at[slot(d, s), rows],
             hid_send.at[d, s, g], hid_recv.at[d, s, g], (near[d], e))

    def ways(s, g):
        return (0, 1) if s < half else ((0,) if g in (0, 3) else (1,))

    def forward_counts(d, s):
        send(("n", d, s), counts.at[owners + slot(d, s - 1)], counts.at[owners + slot(d, s)],
             cnt_send.at[d, s], cnt_recv.at[d, s], (near[d], e))

    def hidden(first, count):
        rows = count * block
        base = first * block
        acc_g[0:rows, :] = jnp.zeros((rows, acc_g.shape[1]), jnp.float32)
        acc_u[0:rows, :] = jnp.zeros((rows, acc_u.shape[1]), jnp.float32)

        def body(j, carry):
            cols = pl.ds(pl.multiple_of(j * step_cols, step_cols), step_cols)
            part = xbuf[base:base + rows, cols]
            dims = (((1,), (1,)), ((), ()))
            acc_g[0:rows, :] += lax.dot_general(part, wg[:, cols], dims, preferred_element_type=jnp.float32)
            acc_u[0:rows, :] += lax.dot_general(part, wu[:, cols], dims, preferred_element_type=jnp.float32)
            return carry

        lax.fori_loop(0, width // step_cols, body, 0)
        gate = acc_g[0:rows, :]
        out = (gate / (1.0 + jnp.exp(-gate)) * acc_u[0:rows, :]).astype(jnp.bfloat16)
        hbuf[0, base:base + rows, :] = out

    def arrange(j):
        for r in range(n):
            own = slot_of[(offsets[j] + offsets[r]) % n]
            mine[r * block:(r + 1) * block, :] = hbuf[0, own * block:(own + 1) * block, :]

    def down(d, s):
        j = slot(d, s)
        if s < half:
            arrange(j)
        part = factor_ref[0:1, 0:1] * lax.dot_general(
            mine[...], hbuf[j], (((0,), (0,)), ((), ())), preferred_element_type=jnp.float32
        )
        place = at((pos + offsets[j]) % n)
        dpart[j] = part
        if len(down_ref.shape) == 2:
            units = down_ref.shape[0]
            target = down_ref.at[:, pl.ds(pl.multiple_of(place * units, units), units)]
        else:
            target = down_ref.at[place]
        copy = pltpu.make_async_copy(dpart.at[j], target, down_sem.at[j])
        copy.start()
        stores.append(copy)

    def keep(first, count):
        rows = pl.ds(first * block, count * block)
        copy = pltpu.make_async_copy(xbuf.at[rows], x_ref.at[rows], out_sem.at[first])
        copy.start()
        stores.append(copy)

    for s in range(1, half + 1):
        for c in range(owners):
            if s == 1:
                if c == owners - 2:
                    held_back = arrive[("x", 0, 0, c)]
                    held_back.wait_send()
                    pending[:] = [copy for copy in pending if copy is not held_back]
                    exchange(owners - 1)
                if c > 0:
                    arrive[("x", 0, 0, c)].wait_recv()
            else:
                if s == 2 and c == 0:
                    arrive[("x", 0, 1, "first")].wait_recv()
                    arrive[("x", 1, 1, "first")].wait_recv()
                arrive[("x", 0, s - 1, c)].wait_recv()
                arrive[("x", 1, s - 1, c)].wait_recv()
            if s == 1 and c == 0:
                pass
            elif s < half:
                forward(0, s, c)
                forward(1, s, c)
            else:
                forward(0 if c < owners // 2 else 1, s, c)
        if s == 1:
            total = counts[0]
            for k in range(1, owners):
                arrive[("c", 0, k)].wait_recv()
                total = total + held_counts[k]
            counts[owners] = total
            forward_counts(0, 1)
            forward_counts(1, 1)
            keep(0, 1)
            for load in loads:
                load.wait()
            hidden(0, 1)
        else:
            arrive[("n", 0, s - 1)].wait_recv()
            arrive[("n", 1, s - 1)].wait_recv()
            forward_counts(0, s)
            if s < half:
                forward_counts(1, s)
            if s == half:
                for g in range(groups - 2):
                    forward_hidden(0, 1, g)
                    forward_hidden(1, 1, g)
            first = slot(0, s - 1)
            keep(first, 2)
            hidden(first, 2)
    if groups > 1:
        forward_hidden(0, 1, groups - 2)
        forward_hidden(1, 1, groups - 2)
    for c in range(owners):
        arrive[("x", 0 if c < owners // 2 else 1, half, c)].wait_recv()
    keep(n - 1, 1)

    def pass_on(s, g):
        for d in ways(s, g):
            arrive[("h", d, s, g)].wait_recv()
        if s < half:
            for d in ways(s + 1, g):
                forward_hidden(d, s + 1, g)

    for g in range(groups - 2):
        pass_on(1, g)
    hidden(n - 1, 1)
    forward_hidden(0, 1, groups - 1)
    forward_hidden(1, 1, groups - 1)
    arrive[("n", 0, half)].wait_recv()
    total = counts[owners]
    for j in range(1, n):
        total = total + counts[owners + j]
    factor_ref[...] = 2.0 / total
    down(0, 0)
    for s in range(1, half + 1):
        if s == half:
            arrange(n - 1)
        for g in range(groups):
            if s > 1 or g >= groups - 2:
                pass_on(s, g)
        if s == 2:
            count = turned_ref.shape[0]
            if count == width // n:
                turned[...] = xbuf[:, pl.ds(pl.multiple_of(me * count, 128), count)].T
                copy = pltpu.make_async_copy(turned, turned_ref, down_sem.at[n])
                copy.start()
                stores.append(copy)
        down(0, s)
        if s < half:
            down(1, s)
    for copy in pending:
        copy.wait_send()
    for copy in stores:
        copy.wait()


def gather(routes_t, slots_t, tokens, gate_rows, up_rows, n, owners):
    width = tokens.shape[1]
    units = gate_rows.shape[0]
    block = owners * CAP
    half = n // 2
    vmem = pl.BlockSpec(memory_space=pltpu.VMEM)
    hbm = pl.BlockSpec(memory_space=pl.ANY)
    rows = n * block
    dma = pltpu.SemaphoreType.DMA
    return pl.pallas_call(
        functools.partial(gather_kernel, n, owners),
        out_shape=(
            jax.ShapeDtypeStruct((rows, width), jnp.bfloat16),
            jax.ShapeDtypeStruct((units, n * units) if units % 128 == 0 else (n, units, units), jnp.float32),
            jax.ShapeDtypeStruct((8, 128), jnp.float32),
            jax.ShapeDtypeStruct((width // n, rows) if (width // n) % 128 == 0 else (8, 128), jnp.bfloat16),
        ),
        in_specs=[vmem, vmem, hbm, hbm, hbm],
        out_specs=(hbm, hbm, vmem, hbm),
        scratch_shapes=[
            pltpu.VMEM((rows, width), jnp.bfloat16),
            pltpu.VMEM((block - CAP, width), jnp.bfloat16),
            pltpu.VMEM(tokens.shape, jnp.bfloat16),
            pltpu.VMEM((units, width), jnp.bfloat16),
            pltpu.VMEM((units, width), jnp.bfloat16),
            pltpu.VMEM((2 * block, units), jnp.float32),
            pltpu.VMEM((2 * block, units), jnp.float32),
            pltpu.VMEM((n, rows, units), jnp.bfloat16),
            pltpu.VMEM((rows, units), jnp.bfloat16),
            pltpu.VMEM((width // n, rows) if (width // n) % 128 == 0 else (8, 128), jnp.bfloat16),
            pltpu.VMEM((n, units, units), jnp.float32),
            pltpu.VMEM((owners + n, 8, 128), jnp.float32),
            pltpu.VMEM((owners, 8, 128), jnp.float32),
            dma((width // (1024 if width % 1024 == 0 else 128),)),
            dma((2,)),
            dma((n,)),
            dma((n + 1,)),
            dma((owners,)),
            dma((owners,)),
            dma((owners,)),
            dma((owners,)),
            dma((2, half + 1, owners)),
            dma((2, half + 1, owners)),
            dma((2, half + 1, 4)),
            dma((2, half + 1, 4)),
            dma((2, half + 1)),
            dma((2, half + 1)),
        ],
        compiler_params=pltpu.CompilerParams(
            collective_id=0, has_side_effects=True, vmem_limit_bytes=60 * 1024 * 1024
        ),
        cost_estimate=pl.CostEstimate(
            flops=4 * rows * width * units, bytes_accessed=6 * rows * width, transcendentals=rows * units
        ),
    )(routes_t, slots_t, tokens, gate_rows, up_rows)


def gram_kernel(tile, pieces, turned_ref, rows_ref, factor_ref, down_in, out_ref, down_out,
                held, parts, turned, down_held, in_sem, out_sem, own_sem):
    width = rows_ref.shape[1]
    slots, count = parts.shape[0], parts.shape[1]
    steps = width // tile
    piece = count // pieces

    def load(j):
        cols = pl.ds(pl.multiple_of(j * tile, tile), tile)
        return pltpu.make_async_copy(rows_ref.at[:, cols], held.at[:, cols], in_sem.at[j])

    def store(j, i):
        b = j % slots
        rows = pl.ds(i * piece, piece)
        cols = pl.ds(pl.multiple_of(j * tile, tile), tile)
        return pltpu.make_async_copy(parts.at[b, rows], out_ref.at[rows, cols], out_sem.at[b, i])

    turned_load = pltpu.make_async_copy(turned_ref, turned, own_sem.at[0])
    down_load = pltpu.make_async_copy(down_in, down_held, own_sem.at[1])
    down_store = pltpu.make_async_copy(down_held, down_out, own_sem.at[2])
    turned_load.start()
    ahead = min(3, steps)
    for j in range(ahead):
        load(j).start()
    turned_load.wait()

    def body(j, carry):
        load(j).wait()

        @pl.when(j + ahead < steps)
        def _():
            load(j + ahead).start()

        @pl.when(j >= slots)
        def _():
            for i in range(pieces):
                store(j - slots, i).wait()

        cols = pl.ds(pl.multiple_of(j * tile, tile), tile)
        for i in range(pieces):
            rows = slice(i * piece, (i + 1) * piece)
            parts[j % slots, rows] = factor_ref[0:1, 0:1] * jnp.dot(
                turned[rows, :], held[:, cols], preferred_element_type=jnp.float32
            )
            store(j, i).start()
        return carry

    early, late = min(slots, steps), max(min(slots, steps), steps - 3)
    lax.fori_loop(0, early, body, 0)
    down_load.start()
    lax.fori_loop(early, late, body, 0)
    down_load.wait()
    down_store.start()
    lax.fori_loop(late, steps, body, 0)
    for j in range(max(0, steps - slots), steps):
        for i in range(pieces):
            store(j, i).wait()
    down_store.wait()


def gram(turned, rows, factor, down):
    depth, width = rows.shape
    count = turned.shape[0]
    tile = 1024 if width % 1024 == 0 else 128
    pieces = 2 if count % 16 == 0 else 1
    slots = 4
    vmem = pl.BlockSpec(memory_space=pltpu.VMEM)
    hbm = pl.BlockSpec(memory_space=pl.ANY)
    dma = pltpu.SemaphoreType.DMA
    return pl.pallas_call(
        functools.partial(gram_kernel, tile, pieces),
        out_shape=(
            jax.ShapeDtypeStruct((count, width), jnp.float32),
            jax.ShapeDtypeStruct(down.shape, jnp.float32),
        ),
        in_specs=[hbm, hbm, vmem, hbm],
        out_specs=(hbm, hbm),
        scratch_shapes=[
            pltpu.VMEM((depth, width), jnp.bfloat16),
            pltpu.VMEM((slots, count, tile), jnp.float32),
            pltpu.VMEM(turned.shape, jnp.bfloat16),
            pltpu.VMEM(down.shape, jnp.float32),
            dma((width // tile,)),
            dma((slots, pieces)),
            dma((3,)),
        ],
        compiler_params=pltpu.CompilerParams(vmem_limit_bytes=60 * 1024 * 1024),
        cost_estimate=pl.CostEstimate(
            flops=2 * depth * count * width, bytes_accessed=4 * count * width, transcendentals=0
        ),
    )(turned, rows, factor, down)


def local(tokens, routes, slot_ids, gate_weight, up_weight):
    width = tokens.shape[1]
    owners = lax.axis_size("expert")
    data_count = lax.axis_size("dp")
    rows, down, factor, turned = gather(
        routes.T, slot_ids.T, tokens, gate_weight[0], up_weight[0], data_count, owners
    )
    count = width // data_count
    if turned.shape[0] != count:
        turned = lax.dynamic_slice_in_dim(rows, lax.axis_index("dp") * count, count, 1).T
    if down.ndim == 3:
        down = jnp.transpose(down, (1, 0, 2)).reshape(down.shape[1], -1)
    input_block, down_block = gram(turned, rows, factor, down)
    return (input_block[None], down_block[None])


def solution(mesh):
    in_specs = (
        P(("dp", "expert"), None),
        P(("dp", "expert"), None),
        P(("dp", "expert"), None),
        P("expert", "dp", None),
        P("expert", "dp", None),
    )
    out_specs = (P("expert", "dp", None), P("expert", "dp", None))
    return jax.shard_map(local, mesh=mesh, in_specs=in_specs, out_specs=out_specs, check_vma=False)
```
